128 devices in a mesh: dp: 64 (over y_lo, x, z, core), ref: 2 (over y_hi).
Axes of the slice: x: 4, y: 4 (y_hi: 2, y_lo: 2; y = y_hi * 2 + y_lo), z: 4, core: 2. Of those that a mesh axis runs over, the one named last changes fastest.
Arguments:
- images: bfloat16 [98304, 1152], P(('dp', 'ref')), may hold values from -100 to 100
- texts: bfloat16 [98304, 1152], P('dp'), may hold values from -100 to 100
- ref_images: bfloat16 [98304, 1152], P(('dp', 'ref')), may hold values from -100 to 100
- ref_texts: bfloat16 [98304, 1152], P('dp', 'ref'), may hold values from -100 to 100
- positives: int32 [64, 1536], P('dp', 'ref'), may hold values from 0 to 1535, each once within a row
- temps: float32 [2], replicated, may hold values from 8 to 16
- biases: float32 [2], replicated, may hold values from -6 to -2
Outputs:
- grad_images: float32 [98304, 1152], P(('dp', 'ref'))
- grad_texts: float32 [98304, 1152], P('dp')
The draws below stay inside these ranges and needn't reach their ends.
Inputs may be any that keep to these rules, and one draw needn't show every extreme that they name: `positives`: row b is a permutation of 0 to 1535.
All inputs are finite; a program needn't handle non-finite values.
Results may differ from the reference program's by a relative error of at most 0.0049.
Values may be sent and summed in bfloat16 or wider, within the bound.
A program may use at most 128 MiB of HBM per device.

```python
import math
import jax
import jax.numpy as jnp
from jax import lax

D = 1152
PAIRS = 1536
BLOCKS = 64
IMAGES = 98304


def scaled_rows(base, key, spread):
    factor = jnp.exp(jax.random.uniform(key, (base.shape[0], 1), jnp.float32) * jnp.log(spread))
    return (base * factor).astype(jnp.bfloat16)


def draw_images(key, part):
    key = jax.random.fold_in(key, 11)
    first, second = jax.random.split(key)
    base = jax.random.normal(first, (IMAGES, D), jnp.float32)
    spread = 10.0
    return scaled_rows(base, second, spread)


def draw_texts(key, part):
    key = jax.random.fold_in(key, 23)
    first, second = jax.random.split(key)
    base = jax.random.normal(first, (IMAGES, D), jnp.float32)
    spread = 10.0
    return scaled_rows(base, second, spread)


def draw_ref_images(key, part):
    key = jax.random.fold_in(key, 37)
    first, second = jax.random.split(key)
    base = jax.random.normal(first, (IMAGES, D), jnp.float32)
    spread = 10.0
    return scaled_rows(base, second, spread)


def draw_ref_texts(key, part):
    key = jax.random.fold_in(key, 41)
    first, second = jax.random.split(key)
    base = jax.random.normal(first, (IMAGES, D), jnp.float32)
    spread = 10.0
    return scaled_rows(base, second, spread)


def setup_inputs(seed: int = 0) -> dict:
    key_of = jax.random.split(jax.random.key(seed), 8)
    images = draw_images(jax.random.fold_in(key_of[7], 71), 0)
    texts = draw_texts(jax.random.fold_in(key_of[7], 71), 0)
    ref_images = draw_ref_images(jax.random.fold_in(key_of[7], 71), 0)
    ref_texts = draw_ref_texts(jax.random.fold_in(key_of[7], 71), 0)
    positives = jax.vmap(lambda own: jax.random.permutation(own, PAIRS))(jax.random.split(key_of[4], BLOCKS)).reshape((BLOCKS, PAIRS)).astype(jnp.int32)
    temps = jnp.clip(jnp.exp(jax.random.uniform(key_of[5], (2,), jnp.float32, math.log(8.0), math.log(16.0))), 8.0, 16.0)
    biases = jnp.clip(jax.random.uniform(key_of[6], (2,), jnp.float32, -6.0, -2.0), -6.0, -2.0)
    return dict(images=images, texts=texts, ref_images=ref_images, ref_texts=ref_texts, positives=positives, temps=temps, biases=biases)


EPS = 1e-06
BETA = 1.0

def unit(values):
    wide = values.astype(jnp.float32)
    length = jnp.sqrt(lax.optimization_barrier(jnp.sum(wide * wide, axis=-1, keepdims=True)) + EPS)
    return (wide / length, length)

def unit_back(grad, direction, length):
    return (grad - direction * lax.optimization_barrier(jnp.sum(grad * direction, axis=-1, keepdims=True))) / length

def slope_of(image_rows, text_rows, ref_image_rows, ref_text_rows, sign, temps, biases):
    dims = (((1,), (1,)), ((), ()))
    logits = temps[0] * lax.dot_general(image_rows, text_rows, dims, preferred_element_type=jnp.float32) + biases[0]
    ref_logits = temps[1] * lax.dot_general(ref_image_rows, ref_text_rows, dims, preferred_element_type=jnp.float32) + biases[1]
    prob = jax.nn.sigmoid(logits)
    slope = -sign * jax.nn.sigmoid(-sign * logits) + BETA * prob * (1.0 - prob) * (logits - ref_logits)
    return slope.astype(jnp.bfloat16)

def back_rows(slope, rows):
    return lax.dot_general(slope, rows, (((0,), (0,)), ((), ())), preferred_element_type=jnp.float32)

def reference(images, texts, ref_images, ref_texts, positives, temps, biases):
    img_blocks = images.reshape(BLOCKS, PAIRS, D)
    txt_blocks = texts.reshape(BLOCKS, PAIRS, D)
    rimg_blocks = ref_images.reshape(BLOCKS, PAIRS, D)
    rtxt_blocks = ref_texts.reshape(BLOCKS, PAIRS, D)
    txt_before = jnp.roll(txt_blocks, 1, axis=0)
    rtxt_before = jnp.roll(rtxt_blocks, 1, axis=0)

    def one_block(item):
        img, txt, txt_prev, rimg, rtxt, rtxt_prev, match = item
        img_dir, img_len = unit(img)
        img_half = img_dir.astype(jnp.bfloat16)
        txt_half = unit(txt)[0].astype(jnp.bfloat16)
        prev_half = unit(txt_prev)[0].astype(jnp.bfloat16)
        rimg_half = unit(rimg)[0].astype(jnp.bfloat16)
        rtxt_half = unit(rtxt)[0].astype(jnp.bfloat16)
        rprev_half = unit(rtxt_prev)[0].astype(jnp.bfloat16)
        columns = jnp.arange(PAIRS, dtype=jnp.int32)
        sign = jnp.where(columns[None, :] == match[:, None], 1.0, -1.0).astype(jnp.float32)
        own = slope_of(img_half, txt_half, rimg_half, rtxt_half, sign, temps, biases)
        after = slope_of(img_half, prev_half, rimg_half, rprev_half, jnp.float32(-1.0), temps, biases)
        img_grad = temps[0] * jnp.dot(own, txt_half, preferred_element_type=jnp.float32) + temps[0] * jnp.dot(after, prev_half, preferred_element_type=jnp.float32)
        grad_img = unit_back(img_grad, img_dir, img_len)
        own_text = temps[0] * back_rows(own, img_half)
        prev_text = temps[0] * back_rows(after, img_half)
        return (grad_img, own_text, prev_text)
    grad_img, own_text, prev_text = lax.map(one_block, (img_blocks, txt_blocks, txt_before, rimg_blocks, rtxt_blocks, rtxt_before, positives))
    text_grad = own_text + jnp.roll(prev_text, -1, axis=0)
    txt_dir, txt_len = unit(txt_blocks)
    grad_txt = unit_back(text_grad, txt_dir, txt_len)
    return (grad_img.reshape(IMAGES, D), grad_txt.reshape(IMAGES, D))
```

```python
import functools

import jax
import jax.numpy as jnp
from jax import lax
from jax.experimental import pallas as pl
from jax.experimental.pallas import tpu as pltpu
from jax.sharding import PartitionSpec as P

EPS = 1e-06
MESH = pl.DeviceIdType.MESH
LOG2E = 1.4426950408889634
F32 = jnp.float32
BF16 = jnp.bfloat16


def row_tiles(rows, tile, body):
    def step(i, carry):
        body(pl.ds(pl.multiple_of(i * tile, tile), tile))
        return carry

    lax.fori_loop(0, rows // tile, step, 0)


def inverse_norm(square_sum):
    return lax.rsqrt(square_sum + EPS)


def row_sum(value):
    return jnp.sum(value, axis=-1, keepdims=True)


def kernel(
    n,
    chunk,
    images,
    texts,
    ref_images,
    ref_texts,
    match,
    temps,
    biases,
    grad_images,
    grad_texts,
    image_raw,
    text_raw,
    ref_raw,
    image_unit,
    ref_unit,
    text_unit,
    ref_text_raw,
    ref_text_unit,
    match_rows,
    logits,
    ref_logits,
    slopes,
    image_sum,
    text_sum,
    text_send,
    text_recv,
    image_send,
    image_recv,
    load_sem,
    half_sem,
    store_sem,
    rt_send_sem,
    rt_recv_sem,
    im_send_sem,
    im_recv_sem,
    tg_send_sem,
    tg_recv_sem,
    ig_send_sem,
    ig_recv_sem,
):
    rows, depth = images.shape
    pairs = texts.shape[0]
    half = ref_texts.shape[1]
    wide = ref_unit.shape[2] // 2
    chunks = pairs // chunk
    tile = 32

    dp, ref = lax.axis_index("dp"), lax.axis_index("ref")
    after, before = lax.rem(dp + 1, n), lax.rem(dp + n - 1, n)
    partner = (dp, 1 - ref)
    next_dev, prev_dev = (after, ref), (before, ref)

    def part(c):
        return pl.ds(pl.multiple_of(c * chunk, chunk), chunk)

    loads = [
        pltpu.make_async_copy(images, image_raw, load_sem.at[0]),
        pltpu.make_async_copy(ref_images, ref_raw.at[0], load_sem.at[1]),
        pltpu.make_async_copy(texts, text_raw, load_sem.at[2]),
        pltpu.make_async_copy(ref_texts, ref_text_raw.at[ref], half_sem),
    ]
    for load in loads:
        load.start()

    barrier = pltpu.get_barrier_semaphore()
    for other in (partner, next_dev, prev_dev):
        pl.semaphore_signal(barrier, inc=1, device_id=other, device_id_type=MESH)
    pl.semaphore_wait(barrier, 3)

    def rt_copy(c):
        return pltpu.make_async_remote_copy(
            src_ref=ref_texts.at[part(c)],
            dst_ref=ref_text_raw.at[ref, part(c)],
            send_sem=rt_send_sem.at[c],
            recv_sem=rt_recv_sem.at[c],
            device_id=partner,
            device_id_type=MESH,
        )

    def tg_copy(c):
        return pltpu.make_async_remote_copy(
            src_ref=text_send.at[part(c)],
            dst_ref=text_recv.at[part(c)],
            send_sem=tg_send_sem.at[c],
            recv_sem=tg_recv_sem.at[c],
            device_id=partner,
            device_id_type=MESH,
        )

    image_copies = [
        pltpu.make_async_remote_copy(
            src_ref=source,
            dst_ref=target,
            send_sem=im_send_sem.at[k],
            recv_sem=im_recv_sem.at[k],
            device_id=prev_dev,
            device_id_type=MESH,
        )
        for k, (source, target) in enumerate(
            ((images, image_unit.at[1]), (ref_images, ref_raw.at[1]))
        )
    ]
    ig_copy = pltpu.make_async_remote_copy(
        src_ref=image_send,
        dst_ref=image_recv,
        send_sem=ig_send_sem,
        recv_sem=ig_recv_sem,
        device_id=next_dev,
        device_id_type=MESH,
    )

    for copy in image_copies:
        copy.start()
    for c in range(chunks):
        rt_copy(c).start()

    gap = wide - half
    if gap:
        for w in range(2):
            for side in range(2):
                ref_unit[w, :, side * wide + half : (side + 1) * wide] = jnp.zeros(
                    (rows, gap), BF16
                )
        for side in range(2):
            ref_text_unit[:, side * wide + half : (side + 1) * wide] = jnp.zeros((pairs, gap), BF16)
    match_rows[...] = jnp.broadcast_to(match[...], (chunk, rows)).T

    def unit_rows(source, target, count):
        def body(at):
            value = source[at, :].astype(F32)
            target[at, :] = (value * inverse_norm(row_sum(value * value))).astype(BF16)

        row_tiles(count, tile, body)

    def unit_ref_rows(w):
        def body(at):
            value = ref_raw[w, at, :].astype(F32)
            value = (value * inverse_norm(row_sum(value * value))).astype(BF16)
            ref_unit[w, at, 0:half] = value[:, 0:half]
            ref_unit[w, at, wide : wide + half] = value[:, half:]

        row_tiles(rows, tile, body)

    def unit_ref_text(c):
        def body(i, carry):
            at = pl.ds(pl.multiple_of(c * chunk + i * tile, tile), tile)
            low, high = ref_text_raw[0, at, :].astype(F32), ref_text_raw[1, at, :].astype(F32)
            scale = inverse_norm(row_sum(low * low) + row_sum(high * high))
            ref_text_unit[at, 0:half] = (low * scale).astype(BF16)
            ref_text_unit[at, wide : wide + half] = (high * scale).astype(BF16)
            return carry

        lax.fori_loop(0, chunk // tile, body, 0)

    t0, t1 = temps[0], temps[1]
    b0, b1 = biases[0], biases[1]
    over_rows = (((1,), (1,)), ((), ()))
    over_images = (((0,), (0,)), ((), ()))

    def window(w, c):
        at = part(c)
        logits[...] = lax.dot_general(
            image_unit[w], text_unit[at, :], over_rows, preferred_element_type=F32
        )
        ref_logits[...] = lax.dot_general(
            ref_unit[w], ref_text_unit[at, :], over_rows, preferred_element_type=F32
        )

        def slope_rows(here):
            policy = logits[here, :] * t0
            gap_to_ref = policy - ref_logits[here, :] * t1 + (b0 - b1)
            growth = jnp.exp2((policy + b0) * (-LOG2E))
            prob = 1.0 / (1.0 + growth)
            rest = growth * prob
            first = prob
            if w == 0:
                columns = lax.broadcasted_iota(jnp.int32, (tile, chunk), 1) + c * chunk
                first = jnp.where(columns == match_rows[here, :], -rest, prob)
            slopes[here, :] = (first + prob * rest * gap_to_ref).astype(BF16)

        row_tiles(rows, tile, slope_rows)
        image_sum[w] += jnp.dot(slopes[...], text_unit[at, :], preferred_element_type=F32)
        return lax.dot_general(
            slopes[...], image_unit[w], over_images, preferred_element_type=F32
        )

    loads[0].wait()
    unit_rows(image_raw, image_unit.at[0], rows)
    loads[1].wait()
    unit_ref_rows(0)
    loads[2].wait()
    unit_rows(text_raw, text_unit, pairs)
    loads[3].wait()
    image_sum[...] = jnp.zeros_like(image_sum)

    def own(c, carry):
        rt_copy(c).wait_recv()
        unit_ref_text(c)
        text_sum[part(c), :] = window(0, c)
        return carry

    lax.fori_loop(0, chunks, own, 0)

    image_copies[0].wait_recv()
    unit_rows(image_unit.at[1], image_unit.at[1], rows)
    image_copies[1].wait_recv()
    unit_ref_rows(1)

    def near(c, carry):
        text_send[part(c), :] = (t0 * (text_sum[part(c), :] + window(1, c))).astype(BF16)
        tg_copy(c).start()
        return carry

    lax.fori_loop(0, chunks, near, 0)

    def cast_rows(at):
        image_send[at, :] = (t0 * image_sum[1, at, :]).astype(BF16)

    row_tiles(rows, tile, cast_rows)
    ig_copy.start()

    def back(grad, value):
        scale = inverse_norm(row_sum(value * value))
        unit = value * scale
        return (grad - unit * row_sum(grad * unit)) * scale

    ig_copy.wait_recv()

    def image_rows(at):
        grad = t0 * image_sum[0, at, :] + image_recv[at, :].astype(F32)
        image_sum[0, at, :] = back(grad, image_raw[at, :].astype(F32))

    row_tiles(rows, tile, image_rows)
    image_store = pltpu.make_async_copy(image_sum.at[0], grad_images, store_sem.at[chunks])
    image_store.start()

    def text_store(c):
        return pltpu.make_async_copy(
            text_sum.at[part(c)], grad_texts.at[part(c)], store_sem.at[c]
        )

    def finish(c, carry):
        tg_copy(c).wait_recv()

        def body(i, inner):
            at = pl.ds(pl.multiple_of(c * chunk + i * tile, tile), tile)
            grad = text_send[at, :].astype(F32) + text_recv[at, :].astype(F32)
            text_sum[at, :] = back(grad, text_raw[at, :].astype(F32))
            return inner

        lax.fori_loop(0, chunk // tile, body, 0)
        text_store(c).start()
        return carry

    lax.fori_loop(0, chunks, finish, 0)
    for copy in image_copies:
        copy.wait_send()
    ig_copy.wait_send()
    image_store.wait()

    def drain(c, carry):
        rt_copy(c).wait_send()
        tg_copy(c).wait_send()
        text_store(c).wait()
        return carry

    lax.fori_loop(0, chunks, drain, 0)


def per_device(n, images, texts, ref_images, ref_texts, positives, temps, biases):
    rows, depth = images.shape
    pairs, half = ref_texts.shape
    wide = -(-half // 128) * 128
    chunk = 256 if pairs % 256 == 0 else pairs // 2
    chunks = pairs // chunk
    anywhere = pl.BlockSpec(memory_space=pl.ANY)
    scalars = pl.BlockSpec(memory_space=pltpu.SMEM)
    dma = pltpu.SemaphoreType.DMA
    return pl.pallas_call(
        functools.partial(kernel, n, chunk),
        out_shape=(
            jax.ShapeDtypeStruct((rows, depth), F32),
            jax.ShapeDtypeStruct((pairs, depth), F32),
        ),
        in_specs=[anywhere] * 4 + [pl.BlockSpec(memory_space=pltpu.VMEM), scalars, scalars],
        out_specs=(anywhere, anywhere),
        scratch_shapes=[
            pltpu.VMEM((rows, depth), BF16),
            pltpu.VMEM((pairs, depth), BF16),
            pltpu.VMEM((2, rows, depth), BF16),
            pltpu.VMEM((2, rows, depth), BF16),
            pltpu.VMEM((2, rows, 2 * wide), BF16),
            pltpu.VMEM((pairs, depth), BF16),
            pltpu.VMEM((2, pairs, half), BF16),
            pltpu.VMEM((pairs, 2 * wide), BF16),
            pltpu.VMEM((rows, chunk), jnp.int32),
            pltpu.VMEM((rows, chunk), F32),
            pltpu.VMEM((rows, chunk), F32),
            pltpu.VMEM((rows, chunk), BF16),
            pltpu.VMEM((2, rows, depth), F32),
            pltpu.VMEM((pairs, depth), F32),
            pltpu.VMEM((pairs, depth), BF16),
            pltpu.VMEM((pairs, depth), BF16),
            pltpu.VMEM((rows, depth), BF16),
            pltpu.VMEM((rows, depth), BF16),
            dma((3,)),
            dma,
            dma((chunks + 1,)),
            dma((chunks,)),
            dma((chunks,)),
            dma((2,)),
            dma((2,)),
            dma((chunks,)),
            dma((chunks,)),
            dma,
            dma,
        ],
        compiler_params=pltpu.CompilerParams(
            collective_id=0, has_side_effects=True, vmem_limit_bytes=62 * 1024 * 1024
        ),
        cost_estimate=pl.CostEstimate(
            flops=16 * rows * pairs * depth,
            bytes_accessed=12 * pairs * depth,
            transcendentals=4 * rows * pairs,
        ),
    )(images, texts, ref_images, ref_texts, positives, temps, biases)


def solution(mesh):
    return jax.shard_map(
        functools.partial(per_device, mesh.shape["dp"]),
        mesh=mesh,
        in_specs=(
            P(("dp", "ref"), None),
            P("dp", None),
            P(("dp", "ref"), None),
            P("dp", "ref"),
            P("dp", "ref"),
            P(),
            P(),
        ),
        out_specs=(P(("dp", "ref"), None), P("dp", None)),
        check_vma=False,
    )
```

```python
import functools

import jax
import jax.numpy as jnp
from jax import lax
from jax.experimental import pallas as pl
from jax.experimental.pallas import tpu as pltpu
from jax.sharding import PartitionSpec as P

EPS = 1e-06
MESH = pl.DeviceIdType.MESH
LOG2E = 1.4426950408889634
F32 = jnp.float32
BF16 = jnp.bfloat16
GROUP = 4

PLANE = 32
OUT_SAME, OUT_OTHER = (3, 5, 7), (1, 9, 17)
BACK_SAME, BACK_OTHER = (26, 28), (14, 22)


def blocks(count, size, body):
    def step(i, carry):
        body(pl.multiple_of(i * size, size))
        return carry

    lax.fori_loop(0, count // size, step, 0)


def inverse_norm(square_sum):
    return lax.rsqrt(square_sum + EPS)


def row_sum(value):
    return jnp.sum(value, axis=-1, keepdims=True)


def kernel(
    n,
    chunk,
    images,
    texts,
    ref_images,
    ref_texts,
    match,
    temps,
    biases,
    grad_images,
    grad_texts,
    image_raw,
    text_raw,
    ref_raw,
    own_units,
    near_units,
    text_unit,
    ref_text,
    ref_scale,
    match_rows,
    logits,
    ref_logits,
    slopes,
    image_sum,
    text_sum,
    text_send,
    text_recv,
    text_out,
    image_send,
    image_recv,
    image_out,
    load_sem,
    half_sem,
    store_sem,
    rt_send_sem,
    rt_recv_sem,
    im_send_sem,
    im_recv_sem,
    tg_send_sem,
    tg_recv_sem,
    ig_send_sem,
    ig_recv_sem,
    relay_out_buf,
    relay_back_buf,
    relay_in_sem,
    relay_fwd_sem,
):
    rows, depth = images.shape
    pairs = texts.shape[0]
    half = ref_texts.shape[0]
    chunks = pairs // chunk
    piece = rows // 3
    tile = 32 if piece % 128 == 0 else 16

    dp, ref = lax.axis_index("dp"), lax.axis_index("ref")
    after, before = lax.rem(dp + 1, n), lax.rem(dp + n - 1, n)
    partner = (dp, 1 - ref)
    next_dev, prev_dev = (after, ref), (before, ref)

    def part(c):
        return pl.ds(pl.multiple_of(c * chunk, chunk), chunk)

    own_half = pl.ds(pl.multiple_of(ref * half, half), half)
    loads = [
        pltpu.make_async_copy(images, image_raw, load_sem.at[0]),
        pltpu.make_async_copy(ref_images, ref_raw, load_sem.at[1]),
        pltpu.make_async_copy(texts, text_raw, load_sem.at[2]),
        pltpu.make_async_copy(ref_texts, ref_text.at[own_half], half_sem),
    ]
    for load in loads:
        load.start()

    relayed = n == 2 * PLANE
    place, plane = lax.rem(dp, PLANE), dp // PLANE
    here, there = plane * PLANE, (1 - plane) * PLANE
    is_first = (place == 0) if relayed else None
    is_last = (place == PLANE - 1) if relayed else None

    def any_place(places):
        return functools.reduce(jnp.logical_or, [place == p for p in places])

    if relayed:
        out_same, out_other = any_place(OUT_SAME), any_place(OUT_OTHER)
        back_same, back_other = any_place(BACK_SAME), any_place(BACK_OTHER)
        is_out, is_back = out_same | out_other, back_same | back_other
        first_dev = (jnp.where(out_same | back_other, here, there), ref)
        last_dev = (jnp.where(out_same | back_other, there, here) + PLANE - 1, ref)
        out_index = jnp.where(out_same, (place - 3) // 2, 3 + place // 8)
        back_index = jnp.where(back_same, (place - 26) // 2, 2 + (place - 14) // 8)
        first_out = [here + p for p in OUT_SAME] + [there + p for p in OUT_OTHER]
        first_back = [there + p for p in BACK_SAME] + [here + p for p in BACK_OTHER]
        last_out = [there + p for p in OUT_SAME] + [here + p for p in OUT_OTHER]
        last_back = [here + p for p in BACK_SAME] + [there + p for p in BACK_OTHER]
        out_part = -(-2 * rows // 7 // 16) * 16
        back_part = -(-rows // 5 // 16) * 16

    barrier = pltpu.get_barrier_semaphore()

    def greet(others):
        for other in others:
            pl.semaphore_signal(barrier, inc=1, device_id=other, device_id_type=MESH)

    greet((partner, next_dev, prev_dev))
    if relayed:
        pl.when(is_first)(lambda: greet([(p, ref) for p in first_out + first_back]))
        pl.when(is_last)(lambda: greet([(p, ref) for p in last_out + last_back]))
        pl.when(is_out | is_back)(lambda: greet((first_dev, last_dev)))
    peers = 3
    if relayed:
        peers = jnp.where(is_first | is_last, 13, jnp.where(is_out | is_back, 5, 3))
    pl.semaphore_wait(barrier, peers)

    def rt_copy(c):
        return pltpu.make_async_remote_copy(
            src_ref=ref_texts.at[:, part(c)],
            dst_ref=ref_text.at[own_half, part(c)],
            send_sem=rt_send_sem.at[c],
            recv_sem=rt_recv_sem.at[c],
            device_id=partner,
            device_id_type=MESH,
        )

    def tg_copy(c):
        return pltpu.make_async_remote_copy(
            src_ref=text_send.at[part(c)],
            dst_ref=text_recv.at[part(c)],
            send_sem=tg_send_sem.at[c],
            recv_sem=tg_recv_sem.at[c],
            device_id=partner,
            device_id_type=MESH,
        )

    def im_copy(k):
        at = pl.ds(k * piece, piece)
        return pltpu.make_async_remote_copy(
            src_ref=own_units.at[at],
            dst_ref=near_units.at[at],
            send_sem=im_send_sem.at[k],
            recv_sem=im_recv_sem.at[k],
            device_id=prev_dev,
            device_id_type=MESH,
        )

    ig_copy = pltpu.make_async_remote_copy(
        src_ref=image_send,
        dst_ref=image_recv,
        send_sem=ig_send_sem.at[0],
        recv_sem=ig_recv_sem.at[0],
        device_id=next_dev,
        device_id_type=MESH,
    )

    if relayed:
        out_to_relay = [
            pltpu.make_async_remote_copy(
                src_ref=own_units.at[pl.ds(m * out_part, out_part)],
                dst_ref=relay_out_buf,
                send_sem=im_send_sem.at[m],
                recv_sem=relay_in_sem,
                device_id=(first_out[m], ref),
                device_id_type=MESH,
            )
            for m in range(6)
        ]
        out_rest = pl.ds(6 * out_part, 2 * rows - 6 * out_part)
        out_direct = pltpu.make_async_remote_copy(
            src_ref=own_units.at[out_rest],
            dst_ref=near_units.at[out_rest],
            send_sem=im_send_sem.at[6],
            recv_sem=im_recv_sem.at[6],
            device_id=prev_dev,
            device_id_type=MESH,
        )

        def out_from_relay(m):
            return pltpu.make_async_remote_copy(
                src_ref=relay_out_buf,
                dst_ref=near_units.at[pl.ds(pl.multiple_of(m * out_part, 16), out_part)],
                send_sem=relay_fwd_sem,
                recv_sem=im_recv_sem.at[m],
                device_id=last_dev,
                device_id_type=MESH,
            )

        back_to_relay = [
            pltpu.make_async_remote_copy(
                src_ref=image_send.at[pl.ds(m * back_part, back_part)],
                dst_ref=relay_back_buf,
                send_sem=ig_send_sem.at[m],
                recv_sem=relay_in_sem,
                device_id=(last_back[m], ref),
                device_id_type=MESH,
            )
            for m in range(4)
        ]
        back_rest = pl.ds(4 * back_part, rows - 4 * back_part)
        back_direct = pltpu.make_async_remote_copy(
            src_ref=image_send.at[back_rest],
            dst_ref=image_recv.at[back_rest],
            send_sem=ig_send_sem.at[4],
            recv_sem=ig_recv_sem.at[4],
            device_id=next_dev,
            device_id_type=MESH,
        )

        def back_from_relay(m):
            return pltpu.make_async_remote_copy(
                src_ref=relay_back_buf,
                dst_ref=image_recv.at[pl.ds(pl.multiple_of(m * back_part, 16), back_part)],
                send_sem=relay_fwd_sem,
                recv_sem=ig_recv_sem.at[m],
                device_id=first_dev,
                device_id_type=MESH,
            )

    for c in range(chunks):
        rt_copy(c).start()

    def unit_rows(source, source_at, target, target_at, count):
        def body(start):
            scales = []
            for j in range(GROUP):
                value = source[pl.ds(source_at + start + j * tile, tile), :].astype(F32)
                scales.append(inverse_norm(row_sum(value * value)))
            for j in range(GROUP):
                value = source[pl.ds(source_at + start + j * tile, tile), :].astype(F32)
                target[pl.ds(target_at + start + j * tile, tile), :] = (value * scales[j]).astype(
                    BF16
                )

        blocks(count, GROUP * tile, body)

    for k in range(6):
        if k % 3 == 0:
            loads[k // 3].wait()
        unit_rows(
            (image_raw, ref_raw)[k // 3], (k % 3) * piece, own_units, k * piece, piece
        )
        if relayed:
            pl.when(jnp.logical_not(is_first))(lambda: im_copy(k).start())
            pl.when(is_first)(lambda: out_to_relay[k].start())
        else:
            im_copy(k).start()
    if relayed:
        pl.when(is_first)(lambda: out_direct.start())

    t0, t1 = temps[0], temps[1]
    b0, b1 = biases[0], biases[1]
    over_rows = (((1,), (1,)), ((), ()))
    over_images = (((0,), (0,)), ((), ()))

    def window(units, w, c):
        at = part(c)
        logits[...] = lax.dot_general(
            units[0:rows, :], text_unit[at, :], over_rows, preferred_element_type=F32
        )
        ref_logits[...] = jnp.dot(
            units[rows : 2 * rows, :], ref_text[:, at], preferred_element_type=F32
        )
        ref_temp = ref_scale[c, 0:1, :] * t1

        def slope_rows(start):
            for j in range(GROUP):
                here = pl.ds(start + j * tile, tile)
                policy = logits[here, :] * t0
                gap = policy - ref_logits[here, :] * ref_temp + (b0 - b1)
                growth = jnp.exp2((policy + b0) * (-LOG2E))
                prob = 1.0 / (1.0 + growth)
                rest = growth * prob
                first = prob
                if w == 0:
                    columns = lax.broadcasted_iota(jnp.int32, (tile, chunk), 1) + c * chunk
                    first = jnp.where(columns == match_rows[here, :], -rest, prob)
                slopes[here, :] = (first + prob * rest * gap).astype(BF16)

        blocks(rows, GROUP * tile, slope_rows)
        image_sum[w] += jnp.dot(slopes[...], text_unit[at, :], preferred_element_type=F32)
        return lax.dot_general(
            slopes[...], units[0:rows, :], over_images, preferred_element_type=F32
        )

    match_rows[...] = jnp.broadcast_to(match[...], (chunk, rows)).T
    image_sum[...] = jnp.zeros_like(image_sum)
    loads[2].wait()
    unit_rows(text_raw, 0, text_unit, 0, pairs)
    loads[3].wait()

    def relay_out():
        out_to_relay[0].wait_recv()
        out_from_relay(out_index).start()

    def relay_back():
        back_to_relay[0].wait_recv()
        back_from_relay(back_index).start()

    def own(c, carry):
        rt_copy(c).wait_recv()
        if relayed:
            pl.when(is_out & (c == 1))(relay_out)
        value = ref_text[:, part(c)].astype(F32)
        scale = inverse_norm(jnp.sum(value * value, axis=0, keepdims=True))
        ref_scale[c] = jnp.broadcast_to(scale, (8, chunk))
        text_sum[part(c), :] = window(own_units, 0, c)
        return carry

    lax.fori_loop(0, chunks, own, 0)

    def wait_pieces():
        for k in range(6):
            im_copy(k).wait_recv()

    def wait_parts():
        for m in range(6):
            out_from_relay(m).wait_recv()
        out_direct.wait_recv()

    if relayed:
        pl.when(is_last)(wait_parts)
        pl.when(jnp.logical_not(is_last))(wait_pieces)
    else:
        wait_pieces()

    def near(c, carry):
        text_send[part(c), :] = (t0 * (text_sum[part(c), :] + window(near_units, 1, c))).astype(
            BF16
        )
        tg_copy(c).start()
        return carry

    lax.fori_loop(0, chunks, near, 0)

    def cast_rows(start):
        at = pl.ds(start, GROUP * tile)
        image_send[at, :] = (t0 * image_sum[1, at, :]).astype(BF16)

    blocks(rows, GROUP * tile, cast_rows)

    def start_back():
        for copy in back_to_relay:
            copy.start()
        back_direct.start()

    def wait_back():
        for m in range(4):
            back_from_relay(m).wait_recv()
        back_direct.wait_recv()

    if relayed:
        pl.when(is_last)(start_back)
        pl.when(jnp.logical_not(is_last))(lambda: ig_copy.start())
        pl.when(is_back)(relay_back)
    else:
        ig_copy.start()

    def back_rows(read_grad, raw, out, start):
        scales, alongs = [], []
        for j in range(GROUP):
            at = pl.ds(start + j * tile, tile)
            value = raw[at, :].astype(F32)
            scales.append(inverse_norm(row_sum(value * value)))
            alongs.append(row_sum(read_grad(at) * value))
        for j in range(GROUP):
            at = pl.ds(start + j * tile, tile)
            scale = scales[j]
            along = alongs[j] * scale * scale
            out[at, :] = ((read_grad(at) - raw[at, :].astype(F32) * along) * scale).astype(BF16)

    if relayed:
        pl.when(is_first)(wait_back)
        pl.when(jnp.logical_not(is_first))(lambda: ig_copy.wait_recv())
    else:
        ig_copy.wait_recv()
    blocks(
        rows,
        GROUP * tile,
        lambda start: back_rows(
            lambda at: t0 * image_sum[0, at, :] + image_recv[at, :].astype(F32),
            image_raw,
            image_out,
            start,
        ),
    )
    image_store = pltpu.make_async_copy(image_out, grad_images, store_sem.at[chunks])
    image_store.start()

    def text_store(c):
        return pltpu.make_async_copy(
            text_out.at[part(c)], grad_texts.at[part(c)], store_sem.at[c]
        )

    def finish(c, carry):
        tg_copy(c).wait_recv()
        blocks(
            chunk,
            GROUP * tile,
            lambda start: back_rows(
                lambda at: text_send[at, :].astype(F32) + text_recv[at, :].astype(F32),
                text_raw,
                text_out,
                pl.multiple_of(c * chunk + start, GROUP * tile),
            ),
        )
        text_store(c).start()
        return carry

    lax.fori_loop(0, chunks, finish, 0)

    def sent_pieces():
        for k in range(6):
            im_copy(k).wait_send()

    def sent_parts():
        for copy in out_to_relay:
            copy.wait_send()
        out_direct.wait_send()

    def sent_back():
        for copy in back_to_relay:
            copy.wait_send()
        back_direct.wait_send()

    if relayed:
        pl.when(is_first)(sent_parts)
        pl.when(jnp.logical_not(is_first))(sent_pieces)
        pl.when(is_last)(sent_back)
        pl.when(jnp.logical_not(is_last))(lambda: ig_copy.wait_send())
        pl.when(is_out)(lambda: out_from_relay(out_index).wait_send())
        pl.when(is_back)(lambda: back_from_relay(back_index).wait_send())
    else:
        sent_pieces()
        ig_copy.wait_send()
    image_store.wait()

    def drain(c, carry):
        rt_copy(c).wait_send()
        tg_copy(c).wait_send()
        text_store(c).wait()
        return carry

    lax.fori_loop(0, chunks, drain, 0)


def per_device(n, images, texts, ref_images, ref_texts, positives, temps, biases):
    rows, depth = images.shape
    pairs, half = ref_texts.shape
    chunk = 256 if pairs % 256 == 0 else pairs // 2
    chunks = pairs // chunk
    anywhere = pl.BlockSpec(memory_space=pl.ANY)
    scalars = pl.BlockSpec(memory_space=pltpu.SMEM)
    dma = pltpu.SemaphoreType.DMA
    grad_images, grad_texts = pl.pallas_call(
        functools.partial(kernel, n, chunk),
        out_shape=(
            jax.ShapeDtypeStruct((rows, depth), BF16),
            jax.ShapeDtypeStruct((pairs, depth), BF16),
        ),
        in_specs=[anywhere] * 4 + [pl.BlockSpec(memory_space=pltpu.VMEM), scalars, scalars],
        out_specs=(anywhere, anywhere),
        scratch_shapes=[
            pltpu.VMEM((rows, depth), BF16),
            pltpu.VMEM((pairs, depth), BF16),
            pltpu.VMEM((rows, depth), BF16),
            pltpu.VMEM((2 * rows, depth), BF16),
            pltpu.VMEM((2 * rows, depth), BF16),
            pltpu.VMEM((pairs, depth), BF16),
            pltpu.VMEM((depth, pairs), BF16),
            pltpu.VMEM((chunks, 8, chunk), F32),
            pltpu.VMEM((rows, chunk), jnp.int32),
            pltpu.VMEM((rows, chunk), F32),
            pltpu.VMEM((rows, chunk), F32),
            pltpu.VMEM((rows, chunk), BF16),
            pltpu.VMEM((2, rows, depth), F32),
            pltpu.VMEM((pairs, depth), F32),
            pltpu.VMEM((pairs, depth), BF16),
            pltpu.VMEM((pairs, depth), BF16),
            pltpu.VMEM((pairs, depth), BF16),
            pltpu.VMEM((rows, depth), BF16),
            pltpu.VMEM((rows, depth), BF16),
            pltpu.VMEM((rows, depth), BF16),
            dma((3,)),
            dma,
            dma((chunks + 1,)),
            dma((chunks,)),
            dma((chunks,)),
            dma((7,)),
            dma((7,)),
            dma((chunks,)),
            dma((chunks,)),
            dma((5,)),
            dma((5,)),
            pltpu.VMEM((-(-2 * rows // 7 // 16) * 16, depth), BF16),
            pltpu.VMEM((-(-rows // 5 // 16) * 16, depth), BF16),
            dma,
            dma,
        ],
        compiler_params=pltpu.CompilerParams(
            collective_id=0, has_side_effects=True, vmem_limit_bytes=62 * 1024 * 1024
        ),
        cost_estimate=pl.CostEstimate(
            flops=16 * rows * pairs * depth,
            bytes_accessed=12 * pairs * depth,
            transcendentals=4 * rows * pairs,
        ),
    )(images, texts, ref_images, ref_texts.T, positives, temps, biases)
    return grad_images.astype(F32), grad_texts.astype(F32)


def solution(mesh):
    return jax.shard_map(
        functools.partial(per_device, mesh.shape["dp"]),
        mesh=mesh,
        in_specs=(
            P(("dp", "ref"), None),
            P("dp", None),
            P(("dp", "ref"), None),
            P("dp", "ref"),
            P("dp", "ref"),
            P(),
            P(),
        ),
        out_specs=(P(("dp", "ref"), None), P("dp", None)),
        check_vma=False,
    )
```

```python
import functools

import jax
import jax.numpy as jnp
from jax import lax
from jax.experimental import pallas as pl
from jax.experimental.pallas import tpu as pltpu
from jax.sharding import PartitionSpec as P

EPS = 1e-06
MESH = pl.DeviceIdType.MESH
LOG2E = 1.4426950408889634
F32 = jnp.float32
BF16 = jnp.bfloat16
GROUP = 4

PLANE = 32
OUT_SAME, OUT_OTHER = (3, 5, 7), (1, 9, 17)
BACK_SAME, BACK_OTHER = (26, 28), (14, 22)


def blocks(count, size, body):
    def step(i, carry):
        body(pl.multiple_of(i * size, size))
        return carry

    lax.fori_loop(0, count // size, step, 0)


def inverse_norm(square_sum):
    return lax.rsqrt(square_sum + EPS)


def row_sum(value):
    return jnp.sum(value, axis=-1, keepdims=True)


def kernel(
    n,
    chunk,
    images,
    texts,
    ref_images,
    ref_texts,
    match,
    temps,
    biases,
    grad_images,
    grad_texts,
    image_raw,
    text_raw,
    ref_raw,
    own_units,
    near_units,
    text_unit,
    ref_text,
    ref_scale,
    match_rows,
    logits,
    ref_logits,
    slopes,
    near_sum,
    text_send,
    text_recv,
    image_send,
    image_recv,
    load_sem,
    half_sem,
    rt_send_sem,
    rt_recv_sem,
    im_send_sem,
    im_recv_sem,
    tg_send_sem,
    tg_recv_sem,
    ig_send_sem,
    ig_recv_sem,
    relay_out_buf,
    relay_back_buf,
    relay_in_sem,
    relay_fwd_sem,
):
    rows, depth = images.shape
    pairs = texts.shape[0]
    half = ref_texts.shape[0]
    chunks = pairs // chunk
    piece = rows // 3
    tile = 32 if piece % 128 == 0 else 16
    early = chunks // 2

    dp, ref = lax.axis_index("dp"), lax.axis_index("ref")
    after, before = lax.rem(dp + 1, n), lax.rem(dp + n - 1, n)
    partner = (dp, 1 - ref)
    next_dev, prev_dev = (after, ref), (before, ref)

    def part(c):
        return pl.ds(pl.multiple_of(c * chunk, chunk), chunk)

    own_half = pl.ds(pl.multiple_of(ref * half, half), half)
    loads = [
        pltpu.make_async_copy(images, image_raw, load_sem.at[0]),
        pltpu.make_async_copy(ref_images, ref_raw, load_sem.at[1]),
        pltpu.make_async_copy(texts, text_raw, load_sem.at[2]),
        pltpu.make_async_copy(ref_texts, ref_text.at[own_half], half_sem),
    ]
    for load in loads:
        load.start()

    relayed = n == 2 * PLANE
    place, plane = lax.rem(dp, PLANE), dp // PLANE
    here, there = plane * PLANE, (1 - plane) * PLANE
    is_first = (place == 0) if relayed else None
    is_last = (place == PLANE - 1) if relayed else None

    def any_place(places):
        return functools.reduce(jnp.logical_or, [place == p for p in places])

    if relayed:
        out_same, out_other = any_place(OUT_SAME), any_place(OUT_OTHER)
        back_same, back_other = any_place(BACK_SAME), any_place(BACK_OTHER)
        is_out, is_back = out_same | out_other, back_same | back_other
        first_dev = (jnp.where(out_same | back_other, here, there), ref)
        last_dev = (jnp.where(out_same | back_other, there, here) + PLANE - 1, ref)
        out_index = jnp.where(out_same, (place - 3) // 2, 3 + place // 8)
        back_index = jnp.where(back_same, (place - 26) // 2, 2 + (place - 14) // 8)
        first_out = [here + p for p in OUT_SAME] + [there + p for p in OUT_OTHER]
        first_back = [there + p for p in BACK_SAME] + [here + p for p in BACK_OTHER]
        last_out = [there + p for p in OUT_SAME] + [here + p for p in OUT_OTHER]
        last_back = [here + p for p in BACK_SAME] + [there + p for p in BACK_OTHER]
        out_part = -(-2 * rows // 7 // 16) * 16
        back_part = -(-rows // 5 // 16) * 16

    barrier = pltpu.get_barrier_semaphore()

    def greet(others):
        for other in others:
            pl.semaphore_signal(barrier, inc=1, device_id=other, device_id_type=MESH)

    greet((partner, next_dev, prev_dev))
    if relayed:
        pl.when(is_first)(lambda: greet([(p, ref) for p in first_out + first_back]))
        pl.when(is_last)(lambda: greet([(p, ref) for p in last_out + last_back]))
        pl.when(is_out | is_back)(lambda: greet((first_dev, last_dev)))
    peers = 3
    if relayed:
        peers = jnp.where(is_first | is_last, 13, jnp.where(is_out | is_back, 5, 3))
    pl.semaphore_wait(barrier, peers)

    def rt_copy(c):
        return pltpu.make_async_remote_copy(
            src_ref=ref_texts.at[:, part(c)],
            dst_ref=ref_text.at[own_half, part(c)],
            send_sem=rt_send_sem.at[c],
            recv_sem=rt_recv_sem.at[c],
            device_id=partner,
            device_id_type=MESH,
        )

    def tg_copy(c):
        return pltpu.make_async_remote_copy(
            src_ref=text_send.at[part(c)],
            dst_ref=text_recv.at[part(c)],
            send_sem=tg_send_sem.at[c],
            recv_sem=tg_recv_sem.at[c],
            device_id=partner,
            device_id_type=MESH,
        )

    def im_copy(k):
        at = pl.ds(k * piece, piece)
        return pltpu.make_async_remote_copy(
            src_ref=own_units.at[at],
            dst_ref=near_units.at[at],
            send_sem=im_send_sem.at[k],
            recv_sem=im_recv_sem.at[k],
            device_id=prev_dev,
            device_id_type=MESH,
        )

    ig_copy = pltpu.make_async_remote_copy(
        src_ref=image_send,
        dst_ref=image_recv,
        send_sem=ig_send_sem.at[0],
        recv_sem=ig_recv_sem.at[0],
        device_id=next_dev,
        device_id_type=MESH,
    )

    if relayed:
        out_to_relay = [
            pltpu.make_async_remote_copy(
                src_ref=own_units.at[pl.ds(m * out_part, out_part)],
                dst_ref=relay_out_buf,
                send_sem=im_send_sem.at[m],
                recv_sem=relay_in_sem,
                device_id=(first_out[m], ref),
                device_id_type=MESH,
            )
            for m in range(6)
        ]
        out_rest = pl.ds(6 * out_part, 2 * rows - 6 * out_part)
        out_direct = pltpu.make_async_remote_copy(
            src_ref=own_units.at[out_rest],
            dst_ref=near_units.at[out_rest],
            send_sem=im_send_sem.at[6],
            recv_sem=im_recv_sem.at[6],
            device_id=prev_dev,
            device_id_type=MESH,
        )

        def out_from_relay(m):
            return pltpu.make_async_remote_copy(
                src_ref=relay_out_buf,
                dst_ref=near_units.at[pl.ds(pl.multiple_of(m * out_part, 16), out_part)],
                send_sem=relay_fwd_sem,
                recv_sem=im_recv_sem.at[m],
                device_id=last_dev,
                device_id_type=MESH,
            )

        back_to_relay = [
            pltpu.make_async_remote_copy(
                src_ref=image_send.at[pl.ds(m * back_part, back_part)],
                dst_ref=relay_back_buf,
                send_sem=ig_send_sem.at[m],
                recv_sem=relay_in_sem,
                device_id=(last_back[m], ref),
                device_id_type=MESH,
            )
            for m in range(4)
        ]
        back_rest = pl.ds(4 * back_part, rows - 4 * back_part)
        back_direct = pltpu.make_async_remote_copy(
            src_ref=image_send.at[back_rest],
            dst_ref=image_recv.at[back_rest],
            send_sem=ig_send_sem.at[4],
            recv_sem=ig_recv_sem.at[4],
            device_id=next_dev,
            device_id_type=MESH,
        )

        def back_from_relay(m):
            return pltpu.make_async_remote_copy(
                src_ref=relay_back_buf,
                dst_ref=image_recv.at[pl.ds(pl.multiple_of(m * back_part, 16), back_part)],
                send_sem=relay_fwd_sem,
                recv_sem=ig_recv_sem.at[m],
                device_id=first_dev,
                device_id_type=MESH,
            )

    for c in range(chunks):
        rt_copy(c).start()

    def unit_rows(source, source_at, target, target_at, count):
        def body(start):
            scales = []
            for j in range(GROUP):
                value = source[pl.ds(source_at + start + j * tile, tile), :].astype(F32)
                scales.append(inverse_norm(row_sum(value * value)))
            for j in range(GROUP):
                value = source[pl.ds(source_at + start + j * tile, tile), :].astype(F32)
                target[pl.ds(target_at + start + j * tile, tile), :] = (value * scales[j]).astype(
                    BF16
                )

        blocks(count, GROUP * tile, body)

    for k in range(6):
        if k % 3 == 0:
            loads[k // 3].wait()
        unit_rows(
            (image_raw, ref_raw)[k // 3], (k % 3) * piece, own_units, k * piece, piece
        )
        if relayed:
            pl.when(jnp.logical_not(is_first))(lambda: im_copy(k).start())
            pl.when(is_first)(lambda: out_to_relay[k].start())
        else:
            im_copy(k).start()
    if relayed:
        pl.when(is_first)(lambda: out_direct.start())

    t0, t1 = temps[0], temps[1]
    b0, b1 = biases[0], biases[1]
    over_rows = (((1,), (1,)), ((), ()))
    over_images = (((0,), (0,)), ((), ()))

    def window(units, w, c):
        at = part(c)
        logits[...] = lax.dot_general(
            units[0:rows, :], text_unit[at, :], over_rows, preferred_element_type=F32
        )
        ref_logits[...] = jnp.dot(
            units[rows : 2 * rows, :], ref_text[:, at], preferred_element_type=F32
        )
        ref_temp = ref_scale[c, 0:1, :] * t1

        def slope_rows(start):
            for j in range(GROUP):
                here = pl.ds(start + j * tile, tile)
                policy = logits[here, :] * t0
                gap = policy - ref_logits[here, :] * ref_temp + (b0 - b1)
                growth = jnp.exp2((policy + b0) * (-LOG2E))
                prob = 1.0 / (1.0 + growth)
                rest = growth * prob
                first = prob
                if w == 0:
                    columns = lax.broadcasted_iota(jnp.int32, (tile, chunk), 1) + c * chunk
                    first = jnp.where(columns == match_rows[here, :], -rest, prob)
                slopes[here, :] = (first + prob * rest * gap).astype(BF16)

        blocks(rows, GROUP * tile, slope_rows)
        total = near_sum if w else grad_images
        total[...] += jnp.dot(slopes[...], text_unit[at, :], preferred_element_type=F32)
        return lax.dot_general(
            slopes[...], units[0:rows, :], over_images, preferred_element_type=F32
        )

    match_rows[...] = jnp.broadcast_to(match[...], (chunk, rows)).T
    near_sum[...] = jnp.zeros_like(near_sum)
    grad_images[...] = jnp.zeros_like(grad_images)
    loads[2].wait()
    unit_rows(text_raw, 0, text_unit, 0, pairs)
    loads[3].wait()

    def relay_out():
        out_to_relay[0].wait_recv()
        out_from_relay(out_index).start()

    def relay_back():
        back_to_relay[0].wait_recv()
        back_from_relay(back_index).start()

    def own(c, carry):
        rt_copy(c).wait_recv()
        if relayed:
            pl.when(is_out & (c == 1))(relay_out)
        value = ref_text[:, part(c)].astype(F32)
        scale = inverse_norm(jnp.sum(value * value, axis=0, keepdims=True))
        ref_scale[c] = jnp.broadcast_to(scale, (8, chunk))
        grad_texts[part(c), :] = window(own_units, 0, c)
        return carry

    lax.fori_loop(0, early, own, 0)

    def wait_pieces():
        for k in range(6):
            im_copy(k).wait_recv()

    def wait_parts():
        for m in range(6):
            out_from_relay(m).wait_recv()
        out_direct.wait_recv()

    if relayed:
        pl.when(is_last)(wait_parts)
        pl.when(jnp.logical_not(is_last))(wait_pieces)
    else:
        wait_pieces()

    def near(c, carry):
        text_send[part(c), :] = (t0 * (grad_texts[part(c), :] + window(near_units, 1, c))).astype(
            BF16
        )
        tg_copy(c).start()

        @pl.when(c + early < chunks)
        def _():
            own(c + early, 0)

        return carry

    lax.fori_loop(0, chunks, near, 0)

    def cast_rows(start):
        at = pl.ds(start, GROUP * tile)
        image_send[at, :] = (t0 * near_sum[at, :]).astype(BF16)

    blocks(rows, GROUP * tile, cast_rows)

    def start_back():
        for copy in back_to_relay:
            copy.start()
        back_direct.start()

    def wait_back():
        for m in range(4):
            back_from_relay(m).wait_recv()
        back_direct.wait_recv()

    if relayed:
        pl.when(is_last)(start_back)
        pl.when(jnp.logical_not(is_last))(lambda: ig_copy.start())
        pl.when(is_back)(relay_back)
    else:
        ig_copy.start()

    def back_rows(read_grad, raw, out, start):
        scales, alongs = [], []
        for j in range(GROUP):
            at = pl.ds(start + j * tile, tile)
            value = raw[at, :].astype(F32)
            scales.append(inverse_norm(row_sum(value * value)))
            alongs.append(row_sum(read_grad(at) * value))
        for j in range(GROUP):
            at = pl.ds(start + j * tile, tile)
            scale = scales[j]
            along = alongs[j] * scale * scale
            out[at, :] = (read_grad(at) - raw[at, :].astype(F32) * along) * scale

    if relayed:
        pl.when(is_first)(wait_back)
        pl.when(jnp.logical_not(is_first))(lambda: ig_copy.wait_recv())
    else:
        ig_copy.wait_recv()
    blocks(
        rows,
        GROUP * tile,
        lambda start: back_rows(
            lambda at: t0 * grad_images[at, :] + image_recv[at, :].astype(F32),
            image_raw,
            grad_images,
            start,
        ),
    )

    def finish(c, carry):
        tg_copy(c).wait_recv()
        blocks(
            chunk,
            GROUP * tile,
            lambda start: back_rows(
                lambda at: text_send[at, :].astype(F32) + text_recv[at, :].astype(F32),
                text_raw,
                grad_texts,
                pl.multiple_of(c * chunk + start, GROUP * tile),
            ),
        )
        return carry

    lax.fori_loop(0, chunks, finish, 0)

    def sent_pieces():
        for k in range(6):
            im_copy(k).wait_send()

    def sent_parts():
        for copy in out_to_relay:
            copy.wait_send()
        out_direct.wait_send()

    def sent_back():
        for copy in back_to_relay:
            copy.wait_send()
        back_direct.wait_send()

    if relayed:
        pl.when(is_first)(sent_parts)
        pl.when(jnp.logical_not(is_first))(sent_pieces)
        pl.when(is_last)(sent_back)
        pl.when(jnp.logical_not(is_last))(lambda: ig_copy.wait_send())
        pl.when(is_out)(lambda: out_from_relay(out_index).wait_send())
        pl.when(is_back)(lambda: back_from_relay(back_index).wait_send())
    else:
        sent_pieces()
        ig_copy.wait_send()

    def drain(c, carry):
        rt_copy(c).wait_send()
        tg_copy(c).wait_send()
        return carry

    lax.fori_loop(0, chunks, drain, 0)


def per_device(n, images, texts, ref_images, ref_texts, positives, temps, biases):
    rows, depth = images.shape
    pairs, half = ref_texts.shape
    chunk = 256 if pairs % 256 == 0 else pairs // 2
    chunks = pairs // chunk
    anywhere = pl.BlockSpec(memory_space=pl.ANY)
    scalars = pl.BlockSpec(memory_space=pltpu.SMEM)
    dma = pltpu.SemaphoreType.DMA
    grad_images, grad_texts = pl.pallas_call(
        functools.partial(kernel, n, chunk),
        out_shape=(
            pltpu.VMEM((rows, depth), F32),
            pltpu.VMEM((pairs, depth), F32),
        ),
        in_specs=[anywhere] * 4 + [pl.BlockSpec(memory_space=pltpu.VMEM), scalars, scalars],
        out_specs=(pl.BlockSpec(memory_space=pltpu.VMEM), pl.BlockSpec(memory_space=pltpu.VMEM)),
        scratch_shapes=[
            pltpu.VMEM((rows, depth), BF16),
            pltpu.VMEM((pairs, depth), BF16),
            pltpu.VMEM((rows, depth), BF16),
            pltpu.VMEM((2 * rows, depth), BF16),
            pltpu.VMEM((2 * rows, depth), BF16),
            pltpu.VMEM((pairs, depth), BF16),
            pltpu.VMEM((depth, pairs), BF16),
            pltpu.VMEM((chunks, 8, chunk), F32),
            pltpu.VMEM((rows, chunk), jnp.int32),
            pltpu.VMEM((rows, chunk), F32),
            pltpu.VMEM((rows, chunk), F32),
            pltpu.VMEM((rows, chunk), BF16),
            pltpu.VMEM((rows, depth), F32),
            pltpu.VMEM((pairs, depth), BF16),
            pltpu.VMEM((pairs, depth), BF16),
            pltpu.VMEM((rows, depth), BF16),
            pltpu.VMEM((rows, depth), BF16),
            dma((3,)),
            dma,
            dma((chunks,)),
            dma((chunks,)),
            dma((7,)),
            dma((7,)),
            dma((chunks,)),
            dma((chunks,)),
            dma((5,)),
            dma((5,)),
            pltpu.VMEM((-(-2 * rows // 7 // 16) * 16, depth), BF16),
            pltpu.VMEM((-(-rows // 5 // 16) * 16, depth), BF16),
            dma,
            dma,
        ],
        compiler_params=pltpu.CompilerParams(
            collective_id=0, has_side_effects=True, vmem_limit_bytes=50 * 1024 * 1024
        ),
        cost_estimate=pl.CostEstimate(
            flops=16 * rows * pairs * depth,
            bytes_accessed=12 * pairs * depth,
            transcendentals=4 * rows * pairs,
        ),
    )(images, texts, ref_images, ref_texts.T, positives, temps, biases)
    return grad_images, grad_texts


def solution(mesh):
    return jax.shard_map(
        functools.partial(per_device, mesh.shape["dp"]),
        mesh=mesh,
        in_specs=(
            P(("dp", "ref"), None),
            P("dp", None),
            P(("dp", "ref"), None),
            P("dp", "ref"),
            P("dp", "ref"),
            P(),
            P(),
        ),
        out_specs=(P(("dp", "ref"), None), P("dp", None)),
        check_vma=False,
    )
```

```python
import functools

import jax
import jax.numpy as jnp
from jax import lax
from jax.experimental import pallas as pl
from jax.experimental.pallas import tpu as pltpu
from jax.sharding import PartitionSpec as P

EPS = 1e-06
MESH = pl.DeviceIdType.MESH
LOG2E = 1.4426950408889634
F32 = jnp.float32
BF16 = jnp.bfloat16
GROUP = 4

PLANE = 32
TWICE, SAME, OTHER = (10, 18, 12, 20), (3, 5, 7), (8, 16)
BACK_SAME, BACK_OTHER = (26, 28), (14, 22)
OUT_PARTS, BACK_PARTS = 9, 4


def blocks(count, size, body):
    def step(i, carry):
        body(pl.multiple_of(i * size, size))
        return carry

    lax.fori_loop(0, count // size, step, 0)


def inverse_norm(square_sum):
    return lax.rsqrt(square_sum + EPS)


def row_sum(value):
    return jnp.sum(value, axis=-1, keepdims=True)


def kernel(
    n,
    chunk,
    images,
    texts,
    ref_images,
    ref_texts,
    match,
    temps,
    biases,
    grad_images,
    grad_texts,
    image_raw,
    text_raw,
    ref_raw,
    own_units,
    near_units,
    text_unit,
    ref_text,
    ref_scale,
    match_rows,
    logits,
    ref_logits,
    slopes,
    near_sum,
    text_send,
    text_recv,
    image_send,
    image_recv,
    load_sem,
    half_sem,
    rt_send_sem,
    rt_recv_sem,
    im_send_sem,
    im_recv_sem,
    tg_send_sem,
    tg_recv_sem,
    ig_send_sem,
    ig_recv_sem,
    relay_out_buf,
    relay_back_buf,
    relay_in_sem,
    relay_fwd_sem,
):
    rows, depth = images.shape
    pairs = texts.shape[0]
    half = ref_texts.shape[0]
    chunks = pairs // chunk
    piece = rows // 3
    tile = 32 if piece % 128 == 0 else 16
    early = chunks // 2

    dp, ref = lax.axis_index("dp"), lax.axis_index("ref")
    after, before = lax.rem(dp + 1, n), lax.rem(dp + n - 1, n)
    partner = (dp, 1 - ref)
    next_dev, prev_dev = (after, ref), (before, ref)

    def part(c):
        return pl.ds(pl.multiple_of(c * chunk, chunk), chunk)

    own_half = pl.ds(pl.multiple_of(ref * half, half), half)
    loads = [
        pltpu.make_async_copy(images, image_raw, load_sem.at[0]),
        pltpu.make_async_copy(ref_images, ref_raw, load_sem.at[1]),
        pltpu.make_async_copy(texts, text_raw, load_sem.at[2]),
        pltpu.make_async_copy(ref_texts, ref_text.at[own_half], half_sem),
    ]
    for load in loads:
        load.start()

    relayed = n == 2 * PLANE
    if relayed:
        place, plane = lax.rem(dp, PLANE), dp // PLANE
        here, there = plane * PLANE, (1 - plane) * PLANE
        is_first, is_last = place == 0, place == PLANE - 1

        def among(places):
            return functools.reduce(jnp.logical_or, [place == p for p in places])

        def order(places, start):
            return sum(jnp.where(place == p, start + i, 0) for i, p in enumerate(places))

        second = tuple(p + 1 for p in TWICE)
        is_pass, is_second = among(TWICE), among(second)
        is_same, is_other = among(SAME), among(OTHER)
        back_same, back_other = among(BACK_SAME), among(BACK_OTHER)
        is_back = back_same | back_other
        is_relay = is_pass | is_second | is_same | is_other | is_back
        source = jnp.where(
            is_pass | is_same,
            here,
            jnp.where(
                is_second,
                there + place - 1,
                jnp.where(
                    is_other,
                    there,
                    jnp.where(back_same, here + PLANE - 1, there + PLANE - 1),
                ),
            ),
        )
        target = jnp.where(
            is_pass,
            there + place + 1,
            jnp.where(
                is_same,
                there + PLANE - 1,
                jnp.where(
                    is_second | is_other, here + PLANE - 1, jnp.where(back_same, there, here)
                ),
            ),
        )
        source_dev, target_dev = (source, ref), (target, ref)
        out_index = order(second, 0) + order(SAME, 4) + order(OTHER, 7)
        back_index = order(BACK_SAME, 0) + order(BACK_OTHER, 2)
        first_out = [here + p for p in TWICE + SAME] + [there + p for p in OTHER]
        first_back = [there + p for p in BACK_SAME] + [here + p for p in BACK_OTHER]
        last_out = [here + p for p in second + OTHER] + [there + p for p in SAME]
        last_back = [here + p for p in BACK_SAME] + [there + p for p in BACK_OTHER]
        out_part = -(-2 * rows // (OUT_PARTS + 1) // 16) * 16
        back_part = -(-rows // 5 // 16) * 16

    barrier = pltpu.get_barrier_semaphore()

    def greet(others):
        for other in others:
            pl.semaphore_signal(barrier, inc=1, device_id=other, device_id_type=MESH)

    greet((partner, next_dev, prev_dev))
    if relayed:
        pl.when(is_first)(lambda: greet([(p, ref) for p in first_out + first_back]))
        pl.when(is_last)(lambda: greet([(p, ref) for p in last_out + last_back]))
        pl.when(is_relay)(lambda: greet((source_dev, target_dev)))
    peers = 3
    if relayed:
        ends = 3 + OUT_PARTS + BACK_PARTS
        peers = jnp.where(is_first | is_last, ends, jnp.where(is_relay, 5, 3))
    pl.semaphore_wait(barrier, peers)

    def rt_copy(c):
        return pltpu.make_async_remote_copy(
            src_ref=ref_texts.at[:, part(c)],
            dst_ref=ref_text.at[own_half, part(c)],
            send_sem=rt_send_sem.at[c],
            recv_sem=rt_recv_sem.at[c],
            device_id=partner,
            device_id_type=MESH,
        )

    def tg_copy(c):
        return pltpu.make_async_remote_copy(
            src_ref=text_send.at[part(c)],
            dst_ref=text_recv.at[part(c)],
            send_sem=tg_send_sem.at[c],
            recv_sem=tg_recv_sem.at[c],
            device_id=partner,
            device_id_type=MESH,
        )

    def im_copy(k):
        at = pl.ds(k * piece, piece)
        return pltpu.make_async_remote_copy(
            src_ref=own_units.at[at],
            dst_ref=near_units.at[at],
            send_sem=im_send_sem.at[k],
            recv_sem=im_recv_sem.at[k],
            device_id=prev_dev,
            device_id_type=MESH,
        )

    ig_copy = pltpu.make_async_remote_copy(
        src_ref=image_send,
        dst_ref=image_recv,
        send_sem=ig_send_sem.at[0],
        recv_sem=ig_recv_sem.at[0],
        device_id=next_dev,
        device_id_type=MESH,
    )

    if relayed:
        out_to_relay = [
            pltpu.make_async_remote_copy(
                src_ref=own_units.at[pl.ds(m * out_part, out_part)],
                dst_ref=relay_out_buf,
                send_sem=im_send_sem.at[m],
                recv_sem=relay_in_sem,
                device_id=(first_out[m], ref),
                device_id_type=MESH,
            )
            for m in range(OUT_PARTS)
        ]
        out_rest = pl.ds(OUT_PARTS * out_part, 2 * rows - OUT_PARTS * out_part)
        out_direct = pltpu.make_async_remote_copy(
            src_ref=own_units.at[out_rest],
            dst_ref=near_units.at[out_rest],
            send_sem=im_send_sem.at[OUT_PARTS],
            recv_sem=im_recv_sem.at[OUT_PARTS],
            device_id=prev_dev,
            device_id_type=MESH,
        )

        def out_from_relay(m):
            return pltpu.make_async_remote_copy(
                src_ref=relay_out_buf,
                dst_ref=near_units.at[pl.ds(pl.multiple_of(m * out_part, 16), out_part)],
                send_sem=relay_fwd_sem,
                recv_sem=im_recv_sem.at[m],
                device_id=target_dev,
                device_id_type=MESH,
            )

        out_pass = pltpu.make_async_remote_copy(
            src_ref=relay_out_buf,
            dst_ref=relay_out_buf,
            send_sem=relay_fwd_sem,
            recv_sem=relay_in_sem,
            device_id=target_dev,
            device_id_type=MESH,
        )

        back_to_relay = [
            pltpu.make_async_remote_copy(
                src_ref=image_send.at[pl.ds(m * back_part, back_part)],
                dst_ref=relay_back_buf,
                send_sem=ig_send_sem.at[m],
                recv_sem=relay_in_sem,
                device_id=(last_back[m], ref),
                device_id_type=MESH,
            )
            for m in range(BACK_PARTS)
        ]
        back_rest = pl.ds(BACK_PARTS * back_part, rows - BACK_PARTS * back_part)
        back_direct = pltpu.make_async_remote_copy(
            src_ref=image_send.at[back_rest],
            dst_ref=image_recv.at[back_rest],
            send_sem=ig_send_sem.at[BACK_PARTS],
            recv_sem=ig_recv_sem.at[BACK_PARTS],
            device_id=next_dev,
            device_id_type=MESH,
        )

        def back_from_relay(m):
            return pltpu.make_async_remote_copy(
                src_ref=relay_back_buf,
                dst_ref=image_recv.at[pl.ds(pl.multiple_of(m * back_part, 16), back_part)],
                send_sem=relay_fwd_sem,
                recv_sem=ig_recv_sem.at[m],
                device_id=target_dev,
                device_id_type=MESH,
            )

    for c in range(chunks):
        rt_copy(c).start()

    def unit_rows(source, source_at, target, target_at, count):
        def body(start):
            scales = []
            for j in range(GROUP):
                value = source[pl.ds(source_at + start + j * tile, tile), :].astype(F32)
                scales.append(inverse_norm(row_sum(value * value)))
            for j in range(GROUP):
                value = source[pl.ds(source_at + start + j * tile, tile), :].astype(F32)
                target[pl.ds(target_at + start + j * tile, tile), :] = (value * scales[j]).astype(
                    BF16
                )

        blocks(count, GROUP * tile, body)

    def send_parts(k):
        for m in range(k * piece // out_part, min((k + 1) * piece // out_part, OUT_PARTS)):
            out_to_relay[m].start()
        if k == 5:
            out_direct.start()

    for k in range(6):
        if k % 3 == 0:
            loads[k // 3].wait()
        unit_rows(
            (image_raw, ref_raw)[k // 3], (k % 3) * piece, own_units, k * piece, piece
        )
        if relayed:
            pl.when(jnp.logical_not(is_first))(lambda: im_copy(k).start())
            pl.when(is_first)(lambda: send_parts(k))
        else:
            im_copy(k).start()

    t0, t1 = temps[0], temps[1]
    b0, b1 = biases[0], biases[1]
    over_rows = (((1,), (1,)), ((), ()))
    over_images = (((0,), (0,)), ((), ()))

    def window(units, w, c):
        at = part(c)
        logits[...] = lax.dot_general(
            units[0:rows, :], text_unit[at, :], over_rows, preferred_element_type=F32
        )
        ref_logits[...] = jnp.dot(
            units[rows : 2 * rows, :], ref_text[:, at], preferred_element_type=F32
        )
        ref_temp = ref_scale[c, 0:1, :] * t1

        def slope_rows(start):
            for j in range(GROUP):
                here = pl.ds(start + j * tile, tile)
                policy = logits[here, :] * t0
                gap = policy - ref_logits[here, :] * ref_temp + (b0 - b1)
                growth = jnp.exp2((policy + b0) * (-LOG2E))
                prob = 1.0 / (1.0 + growth)
                rest = growth * prob
                first = prob
                if w == 0:
                    columns = lax.broadcasted_iota(jnp.int32, (tile, chunk), 1) + c * chunk
                    first = jnp.where(columns == match_rows[here, :], -rest, prob)
                slopes[here, :] = (first + prob * rest * gap).astype(BF16)

        blocks(rows, GROUP * tile, slope_rows)
        total = near_sum if w else grad_images
        total[...] += jnp.dot(slopes[...], text_unit[at, :], preferred_element_type=F32)
        return lax.dot_general(
            slopes[...], units[0:rows, :], over_images, preferred_element_type=F32
        )

    match_rows[...] = jnp.broadcast_to(match[...], (chunk, rows)).T
    near_sum[...] = jnp.zeros_like(near_sum)
    grad_images[...] = jnp.zeros_like(grad_images)
    loads[2].wait()
    unit_rows(text_raw, 0, text_unit, 0, pairs)
    loads[3].wait()

    def relay_pass():
        out_to_relay[0].wait_recv()
        out_pass.start()

    def relay_out():
        out_to_relay[0].wait_recv()
        out_from_relay(out_index).start()

    def relay_back():
        back_to_relay[0].wait_recv()
        back_from_relay(back_index).start()

    def own(c, carry):
        rt_copy(c).wait_recv()
        if relayed:
            pl.when((is_other & (c == 1)) | (is_second & (c == early - 1)))(relay_out)
        value = ref_text[:, part(c)].astype(F32)
        scale = inverse_norm(jnp.sum(value * value, axis=0, keepdims=True))
        ref_scale[c] = jnp.broadcast_to(scale, (8, chunk))
        grad_texts[part(c), :] = window(own_units, 0, c)
        return carry

    if relayed:
        pl.when(is_pass)(relay_pass)
        pl.when(is_same)(relay_out)
    lax.fori_loop(0, early, own, 0)

    def wait_pieces():
        for k in range(6):
            im_copy(k).wait_recv()

    def wait_parts():
        for m in range(OUT_PARTS):
            out_from_relay(m).wait_recv()
        out_direct.wait_recv()

    if relayed:
        pl.when(is_last)(wait_parts)
        pl.when(jnp.logical_not(is_last))(wait_pieces)
    else:
        wait_pieces()

    def near(c, carry):
        text_send[part(c), :] = (t0 * (grad_texts[part(c), :] + window(near_units, 1, c))).astype(
            BF16
        )
        tg_copy(c).start()

        @pl.when(c + early < chunks)
        def _():
            own(c + early, 0)

        return carry

    lax.fori_loop(0, chunks, near, 0)

    def cast_rows(start):
        at = pl.ds(start, GROUP * tile)
        image_send[at, :] = (t0 * near_sum[at, :]).astype(BF16)

    blocks(rows, GROUP * tile, cast_rows)

    def start_back():
        for copy in back_to_relay:
            copy.start()
        back_direct.start()

    def wait_back():
        for m in range(BACK_PARTS):
            back_from_relay(m).wait_recv()
        back_direct.wait_recv()

    if relayed:
        pl.when(is_last)(start_back)
        pl.when(jnp.logical_not(is_last))(lambda: ig_copy.start())
        pl.when(is_back)(relay_back)
    else:
        ig_copy.start()

    def back_rows(read_grad, raw, out, start):
        scales, alongs = [], []
        for j in range(GROUP):
            at = pl.ds(start + j * tile, tile)
            value = raw[at, :].astype(F32)
            scales.append(inverse_norm(row_sum(value * value)))
            alongs.append(row_sum(read_grad(at) * value))
        for j in range(GROUP):
            at = pl.ds(start + j * tile, tile)
            scale = scales[j]
            along = alongs[j] * scale * scale
            out[at, :] = (read_grad(at) - raw[at, :].astype(F32) * along) * scale

    if relayed:
        pl.when(is_first)(wait_back)
        pl.when(jnp.logical_not(is_first))(lambda: ig_copy.wait_recv())
    else:
        ig_copy.wait_recv()
    blocks(
        rows,
        GROUP * tile,
        lambda start: back_rows(
            lambda at: t0 * grad_images[at, :] + image_recv[at, :].astype(F32),
            image_raw,
            grad_images,
            start,
        ),
    )

    def finish(c, carry):
        tg_copy(c).wait_recv()
        blocks(
            chunk,
            GROUP * tile,
            lambda start: back_rows(
                lambda at: text_send[at, :].astype(F32) + text_recv[at, :].astype(F32),
                text_raw,
                grad_texts,
                pl.multiple_of(c * chunk + start, GROUP * tile),
            ),
        )
        return carry

    lax.fori_loop(0, chunks, finish, 0)

    def sent_pieces():
        for k in range(6):
            im_copy(k).wait_send()

    def sent_parts():
        for copy in out_to_relay:
            copy.wait_send()
        out_direct.wait_send()

    def sent_back():
        for copy in back_to_relay:
            copy.wait_send()
        back_direct.wait_send()

    if relayed:
        pl.when(is_first)(sent_parts)
        pl.when(jnp.logical_not(is_first))(sent_pieces)
        pl.when(is_last)(sent_back)
        pl.when(jnp.logical_not(is_last))(lambda: ig_copy.wait_send())
        pl.when(is_pass)(lambda: out_pass.wait_send())
        pl.when(is_same | is_other | is_second)(lambda: out_from_relay(out_index).wait_send())
        pl.when(is_back)(lambda: back_from_relay(back_index).wait_send())
    else:
        sent_pieces()
        ig_copy.wait_send()

    def drain(c, carry):
        rt_copy(c).wait_send()
        tg_copy(c).wait_send()
        return carry

    lax.fori_loop(0, chunks, drain, 0)


def per_device(n, images, texts, ref_images, ref_texts, positives, temps, biases):
    rows, depth = images.shape
    pairs, half = ref_texts.shape
    chunk = 256 if pairs % 256 == 0 else pairs // 2
    chunks = pairs // chunk
    anywhere = pl.BlockSpec(memory_space=pl.ANY)
    scalars = pl.BlockSpec(memory_space=pltpu.SMEM)
    dma = pltpu.SemaphoreType.DMA
    grad_images, grad_texts = pl.pallas_call(
        functools.partial(kernel, n, chunk),
        out_shape=(
            pltpu.VMEM((rows, depth), F32),
            pltpu.VMEM((pairs, depth), F32),
        ),
        in_specs=[anywhere] * 4 + [pl.BlockSpec(memory_space=pltpu.VMEM), scalars, scalars],
        out_specs=(pl.BlockSpec(memory_space=pltpu.VMEM), pl.BlockSpec(memory_space=pltpu.VMEM)),
        scratch_shapes=[
            pltpu.VMEM((rows, depth), BF16),
            pltpu.VMEM((pairs, depth), BF16),
            pltpu.VMEM((rows, depth), BF16),
            pltpu.VMEM((2 * rows, depth), BF16),
            pltpu.VMEM((2 * rows, depth), BF16),
            pltpu.VMEM((pairs, depth), BF16),
            pltpu.VMEM((depth, pairs), BF16),
            pltpu.VMEM((chunks, 8, chunk), F32),
            pltpu.VMEM((rows, chunk), jnp.int32),
            pltpu.VMEM((rows, chunk), F32),
            pltpu.VMEM((rows, chunk), F32),
            pltpu.VMEM((rows, chunk), BF16),
            pltpu.VMEM((rows, depth), F32),
            pltpu.VMEM((pairs, depth), BF16),
            pltpu.VMEM((pairs, depth), BF16),
            pltpu.VMEM((rows, depth), BF16),
            pltpu.VMEM((rows, depth), BF16),
            dma((3,)),
            dma,
            dma((chunks,)),
            dma((chunks,)),
            dma((OUT_PARTS + 1,)),
            dma((OUT_PARTS + 1,)),
            dma((chunks,)),
            dma((chunks,)),
            dma((BACK_PARTS + 1,)),
            dma((BACK_PARTS + 1,)),
            pltpu.VMEM((-(-2 * rows // (OUT_PARTS + 1) // 16) * 16, depth), BF16),
            pltpu.VMEM((-(-rows // 5 // 16) * 16, depth), BF16),
            dma,
            dma,
        ],
        compiler_params=pltpu.CompilerParams(
            collective_id=0, has_side_effects=True, vmem_limit_bytes=50 * 1024 * 1024
        ),
        cost_estimate=pl.CostEstimate(
            flops=16 * rows * pairs * depth,
            bytes_accessed=12 * pairs * depth,
            transcendentals=4 * rows * pairs,
        ),
    )(images, texts, ref_images, ref_texts.T, positives, temps, biases)
    return grad_images, grad_texts


def solution(mesh):
    return jax.shard_map(
        functools.partial(per_device, mesh.shape["dp"]),
        mesh=mesh,
        in_specs=(
            P(("dp", "ref"), None),
            P("dp", None),
            P(("dp", "ref"), None),
            P("dp", "ref"),
            P("dp", "ref"),
            P(),
            P(),
        ),
        out_specs=(P(("dp", "ref"), None), P("dp", None)),
        check_vma=False,
    )
```

```python
import functools

import jax
import jax.numpy as jnp
from jax import lax
from jax.experimental import pallas as pl
from jax.experimental.pallas import tpu as pltpu
from jax.sharding import PartitionSpec as P

EPS = 1e-06
MESH = pl.DeviceIdType.MESH
LOG2E = 1.4426950408889634
F32 = jnp.float32
BF16 = jnp.bfloat16
GROUP = 4

PLANE = 32
TWICE, SAME, OTHER = (10, 18, 12, 20), (3, 5, 7), (8, 16)
BACK_SAME, BACK_OTHER = (26, 28), (14, 22)
OUT_PARTS, BACK_PARTS = 9, 4


def blocks(count, size, body):
    def step(i, carry):
        body(pl.multiple_of(i * size, size))
        return carry

    lax.fori_loop(0, count // size, step, 0)


def inverse_norm(square_sum):
    return lax.rsqrt(square_sum + EPS)


def row_sum(value):
    return jnp.sum(value, axis=-1, keepdims=True)


def kernel(
    n,
    chunk,
    images,
    texts,
    ref_images,
    ref_texts,
    match,
    temps,
    biases,
    grad_images,
    grad_texts,
    image_raw,
    text_raw,
    ref_raw,
    own_units,
    near_units,
    text_unit,
    ref_text,
    ref_scale,
    match_rows,
    logits,
    ref_logits,
    slopes,
    near_sum,
    text_send,
    text_recv,
    image_send,
    image_recv,
    load_sem,
    half_sem,
    rt_send_sem,
    rt_recv_sem,
    im_send_sem,
    im_recv_sem,
    tg_send_sem,
    tg_recv_sem,
    ig_send_sem,
    ig_recv_sem,
    relay_out_buf,
    relay_back_buf,
    relay_in_sem,
    relay_fwd_sem,
):
    rows, depth = images.shape
    pairs = texts.shape[0]
    half = ref_texts.shape[0]
    chunks = pairs // chunk
    piece = rows // 3
    tile = 32 if piece % 128 == 0 else 16
    early = chunks // 2

    dp, ref = lax.axis_index("dp"), lax.axis_index("ref")
    after, before = lax.rem(dp + 1, n), lax.rem(dp + n - 1, n)
    partner = (dp, 1 - ref)
    next_dev, prev_dev = (after, ref), (before, ref)

    def part(c):
        return pl.ds(pl.multiple_of(c * chunk, chunk), chunk)

    own_half = pl.ds(pl.multiple_of(ref * half, half), half)
    loads = [
        pltpu.make_async_copy(images, image_raw, load_sem.at[0]),
        pltpu.make_async_copy(ref_images, ref_raw, load_sem.at[1]),
        pltpu.make_async_copy(texts, text_raw, load_sem.at[2]),
        pltpu.make_async_copy(ref_texts, ref_text.at[own_half], half_sem),
    ]
    relayed = n == 2 * PLANE
    if relayed:
        place, plane = lax.rem(dp, PLANE), dp // PLANE
        here, there = plane * PLANE, (1 - plane) * PLANE
        is_first, is_last = place == 0, place == PLANE - 1

        def among(places):
            return functools.reduce(jnp.logical_or, [place == p for p in places])

        def order(places, start):
            return sum(jnp.where(place == p, start + i, 0) for i, p in enumerate(places))

        second = tuple(p + 1 for p in TWICE)
        is_pass, is_second = among(TWICE), among(second)
        is_same, is_other = among(SAME), among(OTHER)
        back_same, back_other = among(BACK_SAME), among(BACK_OTHER)
        is_back = back_same | back_other
        is_relay = is_pass | is_second | is_same | is_other | is_back
        source = jnp.where(
            is_pass | is_same,
            here,
            jnp.where(
                is_second,
                there + place - 1,
                jnp.where(
                    is_other,
                    there,
                    jnp.where(back_same, here + PLANE - 1, there + PLANE - 1),
                ),
            ),
        )
        target = jnp.where(
            is_pass,
            there + place + 1,
            jnp.where(
                is_same,
                there + PLANE - 1,
                jnp.where(
                    is_second | is_other, here + PLANE - 1, jnp.where(back_same, there, here)
                ),
            ),
        )
        source_dev, target_dev = (source, ref), (target, ref)
        out_index = order(second, 0) + order(SAME, 4) + order(OTHER, 7)
        back_index = order(BACK_SAME, 0) + order(BACK_OTHER, 2)
        first_out = [here + p for p in TWICE + SAME] + [there + p for p in OTHER]
        first_back = [there + p for p in BACK_SAME] + [here + p for p in BACK_OTHER]
        last_out = [here + p for p in second + OTHER] + [there + p for p in SAME]
        last_back = [here + p for p in BACK_SAME] + [there + p for p in BACK_OTHER]
        out_part = -(-2 * rows // (OUT_PARTS + 1) // 16) * 16
        back_part = -(-rows // 5 // 16) * 16

    barrier = pltpu.get_barrier_semaphore()

    def greet(others):
        for other in others:
            pl.semaphore_signal(barrier, inc=1, device_id=other, device_id_type=MESH)

    greet((partner, next_dev, prev_dev))
    if relayed:
        pl.when(is_first)(lambda: greet([(p, ref) for p in first_out + first_back]))
        pl.when(is_last)(lambda: greet([(p, ref) for p in last_out + last_back]))
        pl.when(is_relay)(lambda: greet((source_dev, target_dev)))
    peers = 3
    if relayed:
        ends = 3 + OUT_PARTS + BACK_PARTS
        peers = jnp.where(is_first | is_last, ends, jnp.where(is_relay, 5, 3))
    for load in loads:
        load.start()
    pl.semaphore_wait(barrier, peers)

    def rt_copy(c):
        return pltpu.make_async_remote_copy(
            src_ref=ref_texts.at[:, part(c)],
            dst_ref=ref_text.at[own_half, part(c)],
            send_sem=rt_send_sem.at[c],
            recv_sem=rt_recv_sem.at[c],
            device_id=partner,
            device_id_type=MESH,
        )

    def tg_copy(c):
        return pltpu.make_async_remote_copy(
            src_ref=text_send.at[part(c)],
            dst_ref=text_recv.at[part(c)],
            send_sem=tg_send_sem.at[c],
            recv_sem=tg_recv_sem.at[c],
            device_id=partner,
            device_id_type=MESH,
        )

    def im_copy(k):
        at = pl.ds(k * piece, piece)
        return pltpu.make_async_remote_copy(
            src_ref=own_units.at[at],
            dst_ref=near_units.at[at],
            send_sem=im_send_sem.at[k],
            recv_sem=im_recv_sem.at[k],
            device_id=prev_dev,
            device_id_type=MESH,
        )

    ig_copy = pltpu.make_async_remote_copy(
        src_ref=image_send,
        dst_ref=image_recv,
        send_sem=ig_send_sem.at[0],
        recv_sem=ig_recv_sem.at[0],
        device_id=next_dev,
        device_id_type=MESH,
    )

    if relayed:
        out_to_relay = [
            pltpu.make_async_remote_copy(
                src_ref=own_units.at[pl.ds(m * out_part, out_part)],
                dst_ref=relay_out_buf,
                send_sem=im_send_sem.at[m],
                recv_sem=relay_in_sem,
                device_id=(first_out[m], ref),
                device_id_type=MESH,
            )
            for m in range(OUT_PARTS)
        ]
        out_rest = pl.ds(OUT_PARTS * out_part, 2 * rows - OUT_PARTS * out_part)
        out_direct = pltpu.make_async_remote_copy(
            src_ref=own_units.at[out_rest],
            dst_ref=near_units.at[out_rest],
            send_sem=im_send_sem.at[OUT_PARTS],
            recv_sem=im_recv_sem.at[OUT_PARTS],
            device_id=prev_dev,
            device_id_type=MESH,
        )

        def out_from_relay(m):
            return pltpu.make_async_remote_copy(
                src_ref=relay_out_buf,
                dst_ref=near_units.at[pl.ds(pl.multiple_of(m * out_part, 16), out_part)],
                send_sem=relay_fwd_sem,
                recv_sem=im_recv_sem.at[m],
                device_id=target_dev,
                device_id_type=MESH,
            )

        out_pass = pltpu.make_async_remote_copy(
            src_ref=relay_out_buf,
            dst_ref=relay_out_buf,
            send_sem=relay_fwd_sem,
            recv_sem=relay_in_sem,
            device_id=target_dev,
            device_id_type=MESH,
        )

        back_to_relay = [
            pltpu.make_async_remote_copy(
                src_ref=image_send.at[pl.ds(m * back_part, back_part)],
                dst_ref=relay_back_buf,
                send_sem=ig_send_sem.at[m],
                recv_sem=relay_in_sem,
                device_id=(last_back[m], ref),
                device_id_type=MESH,
            )
            for m in range(BACK_PARTS)
        ]
        back_rest = pl.ds(BACK_PARTS * back_part, rows - BACK_PARTS * back_part)
        back_direct = pltpu.make_async_remote_copy(
            src_ref=image_send.at[back_rest],
            dst_ref=image_recv.at[back_rest],
            send_sem=ig_send_sem.at[BACK_PARTS],
            recv_sem=ig_recv_sem.at[BACK_PARTS],
            device_id=next_dev,
            device_id_type=MESH,
        )

        def back_from_relay(m):
            return pltpu.make_async_remote_copy(
                src_ref=relay_back_buf,
                dst_ref=image_recv.at[pl.ds(pl.multiple_of(m * back_part, 16), back_part)],
                send_sem=relay_fwd_sem,
                recv_sem=ig_recv_sem.at[m],
                device_id=target_dev,
                device_id_type=MESH,
            )

    for c in range(chunks):
        rt_copy(c).start()

    def unit_rows(source, source_at, target, target_at, count):
        def body(start):
            scales = []
            for j in range(GROUP):
                value = source[pl.ds(source_at + start + j * tile, tile), :].astype(F32)
                scales.append(inverse_norm(row_sum(value * value)))
            for j in range(GROUP):
                value = source[pl.ds(source_at + start + j * tile, tile), :].astype(F32)
                target[pl.ds(target_at + start + j * tile, tile), :] = (value * scales[j]).astype(
                    BF16
                )

        blocks(count, GROUP * tile, body)

    def send_parts(k):
        for m in range(k * piece // out_part, min((k + 1) * piece // out_part, OUT_PARTS)):
            out_to_relay[m].start()
        if k == 5:
            out_direct.start()

    for k in range(6):
        if k % 3 == 0:
            loads[k // 3].wait()
        unit_rows(
            (image_raw, ref_raw)[k // 3], (k % 3) * piece, own_units, k * piece, piece
        )
        if relayed:
            pl.when(jnp.logical_not(is_first))(lambda: im_copy(k).start())
            pl.when(is_first)(lambda: send_parts(k))
        else:
            im_copy(k).start()

    t0, t1 = temps[0], temps[1]
    b0, b1 = biases[0], biases[1]
    over_rows = (((1,), (1,)), ((), ()))
    over_images = (((0,), (0,)), ((), ()))

    def window(units, w, c):
        at = part(c)
        logits[...] = lax.dot_general(
            units[0:rows, :], text_unit[at, :], over_rows, preferred_element_type=F32
        )
        ref_logits[...] = jnp.dot(
            units[rows : 2 * rows, :], ref_text[:, at], preferred_element_type=F32
        )
        ref_temp = ref_scale[c, 0:1, :] * t1

        def slope_rows(start):
            for j in range(GROUP):
                here = pl.ds(start + j * tile, tile)
                policy = logits[here, :] * t0
                gap = policy - ref_logits[here, :] * ref_temp + (b0 - b1)
                growth = jnp.exp2((policy + b0) * (-LOG2E))
                prob = 1.0 / (1.0 + growth)
                rest = growth * prob
                first = prob
                if w == 0:
                    columns = lax.broadcasted_iota(jnp.int32, (tile, chunk), 1) + c * chunk
                    first = jnp.where(columns == match_rows[here, :], -rest, prob)
                slopes[here, :] = (first + prob * rest * gap).astype(BF16)

        blocks(rows, GROUP * tile, slope_rows)
        total = near_sum if w else grad_images
        total[...] += jnp.dot(slopes[...], text_unit[at, :], preferred_element_type=F32)
        return lax.dot_general(
            slopes[...], units[0:rows, :], over_images, preferred_element_type=F32
        )

    match_rows[...] = jnp.broadcast_to(match[...], (chunk, rows)).T
    near_sum[...] = jnp.zeros_like(near_sum)
    grad_images[...] = jnp.zeros_like(grad_images)
    loads[2].wait()
    unit_rows(text_raw, 0, text_unit, 0, pairs)
    loads[3].wait()

    def relay_pass():
        out_to_relay[0].wait_recv()
        out_pass.start()

    def relay_out():
        out_to_relay[0].wait_recv()
        out_from_relay(out_index).start()

    def relay_back():
        back_to_relay[0].wait_recv()
        back_from_relay(back_index).start()

    def own(c, carry):
        rt_copy(c).wait_recv()
        if relayed:
            pl.when((is_other & (c == 1)) | (is_second & (c == early - 1)))(relay_out)
        value = ref_text[:, part(c)].astype(F32)
        scale = inverse_norm(jnp.sum(value * value, axis=0, keepdims=True))
        ref_scale[c] = jnp.broadcast_to(scale, (8, chunk))
        grad_texts[part(c), :] = window(own_units, 0, c)
        return carry

    if relayed:
        pl.when(is_pass)(relay_pass)
        pl.when(is_same)(relay_out)
    lax.fori_loop(0, early, own, 0)

    def wait_pieces():
        for k in range(6):
            im_copy(k).wait_recv()

    def wait_parts():
        for m in range(OUT_PARTS):
            out_from_relay(m).wait_recv()
        out_direct.wait_recv()

    if relayed:
        pl.when(is_last)(wait_parts)
        pl.when(jnp.logical_not(is_last))(wait_pieces)
    else:
        wait_pieces()

    def back_rows(read_grad, raw, out, start, divide):
        scales, alongs = [], []
        for j in range(GROUP):
            at = pl.ds(start + j * tile, tile)
            value = raw[at, :].astype(F32)
            scales.append(inverse_norm(row_sum(value * value)))
            alongs.append(row_sum(read_grad(at) * value))
        for j in range(GROUP):
            at = pl.ds(start + j * tile, tile)
            scale = scales[j]
            along = alongs[j] * scale * scale
            grad = read_grad(at) - raw[at, :].astype(F32) * along
            out[at, :] = (grad * scale if divide else grad).astype(out.dtype)

    def near(c, carry):
        grad_texts[part(c), :] = t0 * (grad_texts[part(c), :] + window(near_units, 1, c))
        blocks(
            chunk,
            GROUP * tile,
            lambda start: back_rows(
                lambda at: grad_texts[at, :],
                text_raw,
                text_send,
                pl.multiple_of(c * chunk + start, GROUP * tile),
                False,
            ),
        )
        tg_copy(c).start()

        @pl.when(c + early < chunks)
        def _():
            own(c + early, 0)

        return carry

    lax.fori_loop(0, chunks, near, 0)

    def cast_rows(start):
        at = pl.ds(start, GROUP * tile)
        image_send[at, :] = (t0 * near_sum[at, :]).astype(BF16)

    blocks(rows, GROUP * tile, cast_rows)

    def start_back():
        for copy in back_to_relay:
            copy.start()
        back_direct.start()

    def wait_back():
        for m in range(BACK_PARTS):
            back_from_relay(m).wait_recv()
        back_direct.wait_recv()

    if relayed:
        pl.when(is_last)(start_back)
        pl.when(jnp.logical_not(is_last))(lambda: ig_copy.start())
        pl.when(is_back)(relay_back)
    else:
        ig_copy.start()

    if relayed:
        pl.when(is_first)(wait_back)
        pl.when(jnp.logical_not(is_first))(lambda: ig_copy.wait_recv())
    else:
        ig_copy.wait_recv()
    blocks(
        rows,
        GROUP * tile,
        lambda start: back_rows(
            lambda at: t0 * grad_images[at, :] + image_recv[at, :].astype(F32),
            image_raw,
            grad_images,
            start,
            True,
        ),
    )

    def finish(c, carry):
        tg_copy(c).wait_recv()
        blocks(
            chunk,
            GROUP * tile,
            lambda start: back_rows(
                lambda at: text_send[at, :].astype(F32) + text_recv[at, :].astype(F32),
                text_raw,
                grad_texts,
                pl.multiple_of(c * chunk + start, GROUP * tile),
                True,
            ),
        )
        return carry

    lax.fori_loop(0, chunks, finish, 0)

    def sent_pieces():
        for k in range(6):
            im_copy(k).wait_send()

    def sent_parts():
        for copy in out_to_relay:
            copy.wait_send()
        out_direct.wait_send()

    def sent_back():
        for copy in back_to_relay:
            copy.wait_send()
        back_direct.wait_send()

    if relayed:
        pl.when(is_first)(sent_parts)
        pl.when(jnp.logical_not(is_first))(sent_pieces)
        pl.when(is_last)(sent_back)
        pl.when(jnp.logical_not(is_last))(lambda: ig_copy.wait_send())
        pl.when(is_pass)(lambda: out_pass.wait_send())
        pl.when(is_same | is_other | is_second)(lambda: out_from_relay(out_index).wait_send())
        pl.when(is_back)(lambda: back_from_relay(back_index).wait_send())
    else:
        sent_pieces()
        ig_copy.wait_send()

    def drain(c, carry):
        rt_copy(c).wait_send()
        tg_copy(c).wait_send()
        return carry

    lax.fori_loop(0, chunks, drain, 0)


def write_out(split, images_in, texts_in, images_out, texts_out, sem):
    copies = []
    for source, target in ((texts_in, texts_out), (images_in, images_out)):
        count = source.shape[0] // split
        for i in range(split):
            at = pl.ds(i * count, count)
            copies.append(
                pltpu.make_async_copy(source.at[at], target.at[at], sem.at[len(copies)])
            )
    for copy in copies:
        copy.start()
    for copy in copies:
        copy.wait()


def per_device(n, images, texts, ref_images, ref_texts, positives, temps, biases):
    rows, depth = images.shape
    pairs, half = ref_texts.shape
    chunk = 256 if pairs % 256 == 0 else pairs // 2
    chunks = pairs // chunk
    anywhere = pl.BlockSpec(memory_space=pl.ANY)
    scalars = pl.BlockSpec(memory_space=pltpu.SMEM)
    dma = pltpu.SemaphoreType.DMA
    grad_images, grad_texts = pl.pallas_call(
        functools.partial(kernel, n, chunk),
        out_shape=(
            pltpu.VMEM((rows, depth), F32),
            pltpu.VMEM((pairs, depth), F32),
        ),
        in_specs=[anywhere] * 4 + [pl.BlockSpec(memory_space=pltpu.VMEM), scalars, scalars],
        out_specs=(pl.BlockSpec(memory_space=pltpu.VMEM), pl.BlockSpec(memory_space=pltpu.VMEM)),
        scratch_shapes=[
            pltpu.VMEM((rows, depth), BF16),
            pltpu.VMEM((pairs, depth), BF16),
            pltpu.VMEM((rows, depth), BF16),
            pltpu.VMEM((2 * rows, depth), BF16),
            pltpu.VMEM((2 * rows, depth), BF16),
            pltpu.VMEM((pairs, depth), BF16),
            pltpu.VMEM((depth, pairs), BF16),
            pltpu.VMEM((chunks, 8, chunk), F32),
            pltpu.VMEM((rows, chunk), jnp.int32),
            pltpu.VMEM((rows, chunk), F32),
            pltpu.VMEM((rows, chunk), F32),
            pltpu.VMEM((rows, chunk), BF16),
            pltpu.VMEM((rows, depth), F32),
            pltpu.VMEM((pairs, depth), BF16),
            pltpu.VMEM((pairs, depth), BF16),
            pltpu.VMEM((rows, depth), BF16),
            pltpu.VMEM((rows, depth), BF16),
            dma((3,)),
            dma,
            dma((chunks,)),
            dma((chunks,)),
            dma((OUT_PARTS + 1,)),
            dma((OUT_PARTS + 1,)),
            dma((chunks,)),
            dma((chunks,)),
            dma((BACK_PARTS + 1,)),
            dma((BACK_PARTS + 1,)),
            pltpu.VMEM((-(-2 * rows // (OUT_PARTS + 1) // 16) * 16, depth), BF16),
            pltpu.VMEM((-(-rows // 5 // 16) * 16, depth), BF16),
            dma,
            dma,
        ],
        compiler_params=pltpu.CompilerParams(
            collective_id=0, has_side_effects=True, vmem_limit_bytes=50 * 1024 * 1024
        ),
        cost_estimate=pl.CostEstimate(
            flops=16 * rows * pairs * depth,
            bytes_accessed=12 * pairs * depth,
            transcendentals=4 * rows * pairs,
        ),
    )(images, texts, ref_images, ref_texts.T, positives, temps, biases)
    split = 4
    return pl.pallas_call(
        functools.partial(write_out, split),
        out_shape=(
            jax.ShapeDtypeStruct((rows, depth), F32),
            jax.ShapeDtypeStruct((pairs, depth), F32),
        ),
        in_specs=[pl.BlockSpec(memory_space=pltpu.VMEM)] * 2,
        out_specs=(anywhere, anywhere),
        scratch_shapes=[dma((2 * split,))],
        compiler_params=pltpu.CompilerParams(vmem_limit_bytes=4 * 1024 * 1024),
        cost_estimate=pl.CostEstimate(
            flops=0, bytes_accessed=8 * (rows + pairs) * depth, transcendentals=0
        ),
    )(
        pltpu.with_memory_space_constraint(grad_images, pltpu.VMEM),
        pltpu.with_memory_space_constraint(grad_texts, pltpu.VMEM),
    )


def solution(mesh):
    return jax.shard_map(
        functools.partial(per_device, mesh.shape["dp"]),
        mesh=mesh,
        in_specs=(
            P(("dp", "ref"), None),
            P("dp", None),
            P(("dp", "ref"), None),
            P("dp", "ref"),
            P("dp", "ref"),
            P(),
            P(),
        ),
        out_specs=(P(("dp", "ref"), None), P("dp", None)),
        check_vma=False,
    )
```

```python
import functools

import jax
import jax.numpy as jnp
from jax import lax
from jax.experimental import pallas as pl
from jax.experimental.pallas import tpu as pltpu
from jax.sharding import PartitionSpec as P

EPS = 1e-06
MESH = pl.DeviceIdType.MESH
LOG2E = 1.4426950408889634
F32 = jnp.float32
BF16 = jnp.bfloat16
GROUP = 4
KEEP = 0.0625

PLANE = 32
TWICE, SAME, OTHER = (10, 18, 12, 20), (3, 5, 7), (8, 16)
BACK_SAME, BACK_OTHER = (26, 28), (14, 22)
OUT_PARTS, BACK_PARTS = 9, 4


def blocks(count, size, body):
    def step(i, carry):
        body(pl.multiple_of(i * size, size))
        return carry

    lax.fori_loop(0, count // size, step, 0)


def inverse_norm(square_sum):
    return lax.rsqrt(square_sum + EPS)


def row_sum(value):
    return jnp.sum(value, axis=-1, keepdims=True)


def kernel(
    n,
    chunk,
    images,
    texts,
    ref_images,
    ref_texts,
    match,
    temps,
    biases,
    grad_images,
    grad_texts,
    image_raw,
    text_raw,
    ref_raw,
    own_units,
    near_units,
    text_unit,
    ref_text,
    ref_scale,
    match_rows,
    logits,
    ref_logits,
    slopes,
    near_sum,
    text_send,
    text_recv,
    image_send,
    image_recv,
    load_sem,
    half_sem,
    rt_send_sem,
    rt_recv_sem,
    im_send_sem,
    im_recv_sem,
    tg_send_sem,
    tg_recv_sem,
    ig_send_sem,
    ig_recv_sem,
    relay_out_buf,
    relay_back_buf,
    relay_in_sem,
    relay_fwd_sem,
):
    rows, depth = images.shape
    pairs = texts.shape[0]
    half = ref_texts.shape[0]
    chunks = pairs // chunk
    piece = rows // 3
    tile = 32 if piece % 128 == 0 else 16
    early = chunks // 2

    dp, ref = lax.axis_index("dp"), lax.axis_index("ref")
    after, before = lax.rem(dp + 1, n), lax.rem(dp + n - 1, n)
    partner = (dp, 1 - ref)
    next_dev, prev_dev = (after, ref), (before, ref)

    def part(c):
        return pl.ds(pl.multiple_of(c * chunk, chunk), chunk)

    own_half = pl.ds(pl.multiple_of(ref * half, half), half)
    loads = [
        pltpu.make_async_copy(images, image_raw, load_sem.at[0]),
        pltpu.make_async_copy(ref_images, ref_raw, load_sem.at[1]),
        pltpu.make_async_copy(texts, text_raw, load_sem.at[2]),
        pltpu.make_async_copy(ref_texts, ref_text.at[own_half], half_sem),
    ]
    relayed = n == 2 * PLANE
    if relayed:
        place, plane = lax.rem(dp, PLANE), dp // PLANE
        here, there = plane * PLANE, (1 - plane) * PLANE
        is_first, is_last = place == 0, place == PLANE - 1

        def among(places):
            return functools.reduce(jnp.logical_or, [place == p for p in places])

        def order(places, start):
            return sum(jnp.where(place == p, start + i, 0) for i, p in enumerate(places))

        second = tuple(p + 1 for p in TWICE)
        is_pass, is_second = among(TWICE), among(second)
        is_same, is_other = among(SAME), among(OTHER)
        back_same, back_other = among(BACK_SAME), among(BACK_OTHER)
        is_back = back_same | back_other
        is_relay = is_pass | is_second | is_same | is_other | is_back
        source = jnp.where(
            is_pass | is_same,
            here,
            jnp.where(
                is_second,
                there + place - 1,
                jnp.where(
                    is_other,
                    there,
                    jnp.where(back_same, here + PLANE - 1, there + PLANE - 1),
                ),
            ),
        )
        target = jnp.where(
            is_pass,
            there + place + 1,
            jnp.where(
                is_same,
                there + PLANE - 1,
                jnp.where(
                    is_second | is_other, here + PLANE - 1, jnp.where(back_same, there, here)
                ),
            ),
        )
        source_dev, target_dev = (source, ref), (target, ref)
        out_index = order(second, 0) + order(SAME, 4) + order(OTHER, 7)
        back_index = order(BACK_SAME, 0) + order(BACK_OTHER, 2)
        first_out = [here + p for p in TWICE + SAME] + [there + p for p in OTHER]
        first_back = [there + p for p in BACK_SAME] + [here + p for p in BACK_OTHER]
        last_out = [here + p for p in second + OTHER] + [there + p for p in SAME]
        last_back = [here + p for p in BACK_SAME] + [there + p for p in BACK_OTHER]
        out_part = -(-2 * rows // (OUT_PARTS + 1) // 16) * 16
        back_part = -(-rows // 5 // 16) * 16

    barrier = pltpu.get_barrier_semaphore()

    def greet(others):
        for other in others:
            pl.semaphore_signal(barrier, inc=1, device_id=other, device_id_type=MESH)

    greet((partner, next_dev, prev_dev))
    if relayed:
        pl.when(is_first)(lambda: greet([(p, ref) for p in first_out + first_back]))
        pl.when(is_last)(lambda: greet([(p, ref) for p in last_out + last_back]))
        pl.when(is_relay)(lambda: greet((source_dev, target_dev)))
    peers = 3
    if relayed:
        ends = 3 + OUT_PARTS + BACK_PARTS
        peers = jnp.where(is_first | is_last, ends, jnp.where(is_relay, 5, 3))
    for load in loads:
        load.start()
    pl.semaphore_wait(barrier, peers)

    def rt_copy(c):
        return pltpu.make_async_remote_copy(
            src_ref=ref_texts.at[:, part(c)],
            dst_ref=ref_text.at[own_half, part(c)],
            send_sem=rt_send_sem.at[c],
            recv_sem=rt_recv_sem.at[c],
            device_id=partner,
            device_id_type=MESH,
        )

    def tg_copy(c):
        return pltpu.make_async_remote_copy(
            src_ref=text_send.at[part(c)],
            dst_ref=text_recv.at[part(c)],
            send_sem=tg_send_sem.at[c],
            recv_sem=tg_recv_sem.at[c],
            device_id=partner,
            device_id_type=MESH,
        )

    def im_copy(k):
        at = pl.ds(k * piece, piece)
        return pltpu.make_async_remote_copy(
            src_ref=own_units.at[at],
            dst_ref=near_units.at[at],
            send_sem=im_send_sem.at[k],
            recv_sem=im_recv_sem.at[k],
            device_id=prev_dev,
            device_id_type=MESH,
        )

    ig_copy = pltpu.make_async_remote_copy(
        src_ref=image_send,
        dst_ref=image_recv,
        send_sem=ig_send_sem.at[0],
        recv_sem=ig_recv_sem.at[0],
        device_id=next_dev,
        device_id_type=MESH,
    )

    if relayed:
        out_to_relay = [
            pltpu.make_async_remote_copy(
                src_ref=own_units.at[pl.ds(m * out_part, out_part)],
                dst_ref=relay_out_buf,
                send_sem=im_send_sem.at[m],
                recv_sem=relay_in_sem,
                device_id=(first_out[m], ref),
                device_id_type=MESH,
            )
            for m in range(OUT_PARTS)
        ]
        out_rest = pl.ds(OUT_PARTS * out_part, 2 * rows - OUT_PARTS * out_part)
        out_direct = pltpu.make_async_remote_copy(
            src_ref=own_units.at[out_rest],
            dst_ref=near_units.at[out_rest],
            send_sem=im_send_sem.at[OUT_PARTS],
            recv_sem=im_recv_sem.at[OUT_PARTS],
            device_id=prev_dev,
            device_id_type=MESH,
        )

        def out_from_relay(m):
            return pltpu.make_async_remote_copy(
                src_ref=relay_out_buf,
                dst_ref=near_units.at[pl.ds(pl.multiple_of(m * out_part, 16), out_part)],
                send_sem=relay_fwd_sem,
                recv_sem=im_recv_sem.at[m],
                device_id=target_dev,
                device_id_type=MESH,
            )

        out_pass = pltpu.make_async_remote_copy(
            src_ref=relay_out_buf,
            dst_ref=relay_out_buf,
            send_sem=relay_fwd_sem,
            recv_sem=relay_in_sem,
            device_id=target_dev,
            device_id_type=MESH,
        )

        back_to_relay = [
            pltpu.make_async_remote_copy(
                src_ref=image_send.at[pl.ds(m * back_part, back_part)],
                dst_ref=relay_back_buf,
                send_sem=ig_send_sem.at[m],
                recv_sem=relay_in_sem,
                device_id=(last_back[m], ref),
                device_id_type=MESH,
            )
            for m in range(BACK_PARTS)
        ]
        back_rest = pl.ds(BACK_PARTS * back_part, rows - BACK_PARTS * back_part)
        back_direct = pltpu.make_async_remote_copy(
            src_ref=image_send.at[back_rest],
            dst_ref=image_recv.at[back_rest],
            send_sem=ig_send_sem.at[BACK_PARTS],
            recv_sem=ig_recv_sem.at[BACK_PARTS],
            device_id=next_dev,
            device_id_type=MESH,
        )

        def back_from_relay(m):
            return pltpu.make_async_remote_copy(
                src_ref=relay_back_buf,
                dst_ref=image_recv.at[pl.ds(pl.multiple_of(m * back_part, 16), back_part)],
                send_sem=relay_fwd_sem,
                recv_sem=ig_recv_sem.at[m],
                device_id=target_dev,
                device_id_type=MESH,
            )

    for c in range(chunks):
        rt_copy(c).start()

    def unit_rows(source, source_at, target, target_at, count):
        def body(start):
            scales = []
            for j in range(GROUP):
                value = source[pl.ds(source_at + start + j * tile, tile), :].astype(F32)
                scales.append(inverse_norm(row_sum(value * value)))
            for j in range(GROUP):
                value = source[pl.ds(source_at + start + j * tile, tile), :].astype(F32)
                target[pl.ds(target_at + start + j * tile, tile), :] = (value * scales[j]).astype(
                    BF16
                )

        blocks(count, GROUP * tile, body)

    def send_parts(k):
        for m in range(k * piece // out_part, min((k + 1) * piece // out_part, OUT_PARTS)):
            out_to_relay[m].start()
        if k == 5:
            out_direct.start()

    for k in range(6):
        if k % 3 == 0:
            loads[k // 3].wait()
        unit_rows(
            (image_raw, ref_raw)[k // 3], (k % 3) * piece, own_units, k * piece, piece
        )
        if relayed:
            pl.when(jnp.logical_not(is_first))(lambda: im_copy(k).start())
            pl.when(is_first)(lambda: send_parts(k))
        else:
            im_copy(k).start()

    t0, t1 = temps[0], temps[1]
    b0, b1 = biases[0], biases[1]
    over_rows = (((1,), (1,)), ((), ()))
    over_images = (((0,), (0,)), ((), ()))

    def window(units, w, c):
        at = part(c)
        logits[...] = lax.dot_general(
            units[0:rows, :], text_unit[at, :], over_rows, preferred_element_type=F32
        )
        ref_logits[...] = jnp.dot(
            units[rows : 2 * rows, :], ref_text[:, at], preferred_element_type=F32
        )
        ref_temp = ref_scale[c, 0:1, :] * t1

        def slope_rows(start):
            for j in range(GROUP):
                here = pl.ds(start + j * tile, tile)
                policy = logits[here, :] * t0
                gap = policy - ref_logits[here, :] * ref_temp + (b0 - b1)
                growth = jnp.exp2((policy + b0) * (-LOG2E))
                prob = 1.0 / (1.0 + growth)
                rest = growth * prob
                first = prob
                if w == 0:
                    columns = lax.broadcasted_iota(jnp.int32, (tile, chunk), 1) + c * chunk
                    first = jnp.where(columns == match_rows[here, :], -rest, prob)
                slopes[here, :] = (first + prob * rest * gap).astype(BF16)

        blocks(rows, GROUP * tile, slope_rows)
        total = near_sum if w else grad_images
        total[...] += jnp.dot(slopes[...], text_unit[at, :], preferred_element_type=F32)
        return lax.dot_general(
            slopes[...], units[0:rows, :], over_images, preferred_element_type=F32
        )

    match_rows[...] = jnp.broadcast_to(match[...], (chunk, rows)).T
    near_sum[...] = jnp.zeros_like(near_sum)
    grad_images[...] = jnp.zeros_like(grad_images)
    loads[2].wait()
    unit_rows(text_raw, 0, text_unit, 0, pairs)
    loads[3].wait()

    def relay_pass():
        out_to_relay[0].wait_recv()
        out_pass.start()

    def relay_out():
        out_to_relay[0].wait_recv()
        out_from_relay(out_index).start()

    def relay_back():
        back_to_relay[0].wait_recv()
        back_from_relay(back_index).start()

    def own(c, carry):
        rt_copy(c).wait_recv()
        if relayed:
            pl.when((is_other & (c == 1)) | (is_second & (c == early - 1)))(relay_out)
        value = ref_text[:, part(c)].astype(F32)
        scale = inverse_norm(jnp.sum(value * value, axis=0, keepdims=True))
        ref_scale[c] = jnp.broadcast_to(scale, (8, chunk))
        grad_texts[part(c), :] = window(own_units, 0, c)
        return carry

    if relayed:
        pl.when(is_pass)(relay_pass)
        pl.when(is_same)(relay_out)
    lax.fori_loop(0, early, own, 0)

    def wait_pieces():
        for k in range(6):
            im_copy(k).wait_recv()

    def wait_parts():
        for m in range(OUT_PARTS):
            out_from_relay(m).wait_recv()
        out_direct.wait_recv()

    if relayed:
        pl.when(is_last)(wait_parts)
        pl.when(jnp.logical_not(is_last))(wait_pieces)
    else:
        wait_pieces()

    def back_rows(read_grad, raw, out, start, divide):
        scales, alongs = [], []
        for j in range(GROUP):
            at = pl.ds(start + j * tile, tile)
            value = raw[at, :].astype(F32)
            scales.append(inverse_norm(row_sum(value * value)))
            alongs.append(row_sum(read_grad(at) * value))
        for j in range(GROUP):
            at = pl.ds(start + j * tile, tile)
            scale = scales[j]
            along = alongs[j] * scale * scale
            grad = read_grad(at) - raw[at, :].astype(F32) * along
            out[at, :] = (grad * scale if divide else grad).astype(out.dtype)

    def near(c, carry):
        grad_texts[part(c), :] = t0 * (grad_texts[part(c), :] + window(near_units, 1, c))
        blocks(
            chunk,
            GROUP * tile,
            lambda start: back_rows(
                lambda at: grad_texts[at, :],
                text_raw,
                text_send,
                pl.multiple_of(c * chunk + start, GROUP * tile),
                False,
            ),
        )
        tg_copy(c).start()

        @pl.when(c + early < chunks)
        def _():
            own(c + early, 0)

        return carry

    lax.fori_loop(0, chunks, near, 0)

    def cast_rows(start):
        for j in range(GROUP):
            at = pl.ds(start + j * tile, tile)
            grad = t0 * near_sum[at, :]
            unit = near_units[at, :].astype(F32)
            along = row_sum(grad * unit)
            image_send[at, :] = (grad - unit * (along * (1.0 - KEEP))).astype(BF16)

    def received(at):
        grad = image_recv[at, :].astype(F32)
        unit = own_units[at, :].astype(F32)
        return grad + unit * (row_sum(grad * unit) * (1.0 / KEEP - 1.0))

    blocks(rows, GROUP * tile, cast_rows)

    def start_back():
        for copy in back_to_relay:
            copy.start()
        back_direct.start()

    def wait_back():
        for m in range(BACK_PARTS):
            back_from_relay(m).wait_recv()
        back_direct.wait_recv()

    if relayed:
        pl.when(is_last)(start_back)
        pl.when(jnp.logical_not(is_last))(lambda: ig_copy.start())
        pl.when(is_back)(relay_back)
    else:
        ig_copy.start()

    if relayed:
        pl.when(is_first)(wait_back)
        pl.when(jnp.logical_not(is_first))(lambda: ig_copy.wait_recv())
    else:
        ig_copy.wait_recv()
    blocks(
        rows,
        GROUP * tile,
        lambda start: back_rows(
            lambda at: t0 * grad_images[at, :] + received(at),
            image_raw,
            grad_images,
            start,
            True,
        ),
    )

    def finish(c, carry):
        tg_copy(c).wait_recv()
        blocks(
            chunk,
            GROUP * tile,
            lambda start: back_rows(
                lambda at: text_send[at, :].astype(F32) + text_recv[at, :].astype(F32),
                text_raw,
                grad_texts,
                pl.multiple_of(c * chunk + start, GROUP * tile),
                True,
            ),
        )
        return carry

    lax.fori_loop(0, chunks, finish, 0)

    def sent_pieces():
        for k in range(6):
            im_copy(k).wait_send()

    def sent_parts():
        for copy in out_to_relay:
            copy.wait_send()
        out_direct.wait_send()

    def sent_back():
        for copy in back_to_relay:
            copy.wait_send()
        back_direct.wait_send()

    if relayed:
        pl.when(is_first)(sent_parts)
        pl.when(jnp.logical_not(is_first))(sent_pieces)
        pl.when(is_last)(sent_back)
        pl.when(jnp.logical_not(is_last))(lambda: ig_copy.wait_send())
        pl.when(is_pass)(lambda: out_pass.wait_send())
        pl.when(is_same | is_other | is_second)(lambda: out_from_relay(out_index).wait_send())
        pl.when(is_back)(lambda: back_from_relay(back_index).wait_send())
    else:
        sent_pieces()
        ig_copy.wait_send()

    def drain(c, carry):
        rt_copy(c).wait_send()
        tg_copy(c).wait_send()
        return carry

    lax.fori_loop(0, chunks, drain, 0)


def write_out(split, images_in, texts_in, images_out, texts_out, sem):
    copies = []
    for source, target in ((texts_in, texts_out), (images_in, images_out)):
        count = source.shape[0] // split
        for i in range(split):
            at = pl.ds(i * count, count)
            copies.append(
                pltpu.make_async_copy(source.at[at], target.at[at], sem.at[len(copies)])
            )
    for copy in copies:
        copy.start()
    for copy in copies:
        copy.wait()


def per_device(n, images, texts, ref_images, ref_texts, positives, temps, biases):
    rows, depth = images.shape
    pairs, half = ref_texts.shape
    chunk = 256 if pairs % 256 == 0 else pairs // 2
    chunks = pairs // chunk
    anywhere = pl.BlockSpec(memory_space=pl.ANY)
    scalars = pl.BlockSpec(memory_space=pltpu.SMEM)
    dma = pltpu.SemaphoreType.DMA
    grad_images, grad_texts = pl.pallas_call(
        functools.partial(kernel, n, chunk),
        out_shape=(
            pltpu.VMEM((rows, depth), F32),
            pltpu.VMEM((pairs, depth), F32),
        ),
        in_specs=[anywhere] * 4 + [pl.BlockSpec(memory_space=pltpu.VMEM), scalars, scalars],
        out_specs=(pl.BlockSpec(memory_space=pltpu.VMEM), pl.BlockSpec(memory_space=pltpu.VMEM)),
        scratch_shapes=[
            pltpu.VMEM((rows, depth), BF16),
            pltpu.VMEM((pairs, depth), BF16),
            pltpu.VMEM((rows, depth), BF16),
            pltpu.VMEM((2 * rows, depth), BF16),
            pltpu.VMEM((2 * rows, depth), BF16),
            pltpu.VMEM((pairs, depth), BF16),
            pltpu.VMEM((depth, pairs), BF16),
            pltpu.VMEM((chunks, 8, chunk), F32),
            pltpu.VMEM((rows, chunk), jnp.int32),
            pltpu.VMEM((rows, chunk), F32),
            pltpu.VMEM((rows, chunk), F32),
            pltpu.VMEM((rows, chunk), BF16),
            pltpu.VMEM((rows, depth), F32),
            pltpu.VMEM((pairs, depth), BF16),
            pltpu.VMEM((pairs, depth), BF16),
            pltpu.VMEM((rows, depth), BF16),
            pltpu.VMEM((rows, depth), BF16),
            dma((3,)),
            dma,
            dma((chunks,)),
            dma((chunks,)),
            dma((OUT_PARTS + 1,)),
            dma((OUT_PARTS + 1,)),
            dma((chunks,)),
            dma((chunks,)),
            dma((BACK_PARTS + 1,)),
            dma((BACK_PARTS + 1,)),
            pltpu.VMEM((-(-2 * rows // (OUT_PARTS + 1) // 16) * 16, depth), BF16),
            pltpu.VMEM((-(-rows // 5 // 16) * 16, depth), BF16),
            dma,
            dma,
        ],
        compiler_params=pltpu.CompilerParams(
            collective_id=0, has_side_effects=True, vmem_limit_bytes=50 * 1024 * 1024
        ),
        cost_estimate=pl.CostEstimate(
            flops=16 * rows * pairs * depth,
            bytes_accessed=12 * pairs * depth,
            transcendentals=4 * rows * pairs,
        ),
    )(images, texts, ref_images, ref_texts.T, positives, temps, biases)
    split = 4
    return pl.pallas_call(
        functools.partial(write_out, split),
        out_shape=(
            jax.ShapeDtypeStruct((rows, depth), F32),
            jax.ShapeDtypeStruct((pairs, depth), F32),
        ),
        in_specs=[pl.BlockSpec(memory_space=pltpu.VMEM)] * 2,
        out_specs=(anywhere, anywhere),
        scratch_shapes=[dma((2 * split,))],
        compiler_params=pltpu.CompilerParams(vmem_limit_bytes=4 * 1024 * 1024),
        cost_estimate=pl.CostEstimate(
            flops=0, bytes_accessed=8 * (rows + pairs) * depth, transcendentals=0
        ),
    )(
        pltpu.with_memory_space_constraint(grad_images, pltpu.VMEM),
        pltpu.with_memory_space_constraint(grad_texts, pltpu.VMEM),
    )


def solution(mesh):
    return jax.shard_map(
        functools.partial(per_device, mesh.shape["dp"]),
        mesh=mesh,
        in_specs=(
            P(("dp", "ref"), None),
            P("dp", None),
            P(("dp", "ref"), None),
            P("dp", "ref"),
            P("dp", "ref"),
            P(),
            P(),
        ),
        out_specs=(P(("dp", "ref"), None), P("dp", None)),
        check_vma=False,
    )
```

```python
import functools

import jax
import jax.numpy as jnp
from jax import lax
from jax.experimental import pallas as pl
from jax.experimental.pallas import tpu as pltpu
from jax.sharding import PartitionSpec as P

EPS = 1e-06
MESH = pl.DeviceIdType.MESH
LOG2E = 1.4426950408889634
F32 = jnp.float32
BF16 = jnp.bfloat16
GROUP = 4
KEEP = 0.0625

PLANE = 32
TWICE, SAME, OTHER = (10, 18, 12, 20), (3, 5, 7), (8, 16)
BACK_SAME, BACK_OTHER = (24, 26, 28), (14, 22)
OUT_PARTS, BACK_PARTS = 9, 5


def blocks(count, size, body):
    def step(i, carry):
        body(pl.multiple_of(i * size, size))
        return carry

    lax.fori_loop(0, count // size, step, 0)


def inverse_norm(square_sum):
    return lax.rsqrt(square_sum + EPS)


def row_sum(value):
    return jnp.sum(value, axis=-1, keepdims=True)


def kernel(
    n,
    chunk,
    images,
    texts,
    ref_images,
    ref_texts,
    match,
    temps,
    biases,
    grad_images,
    grad_texts,
    image_raw,
    text_raw,
    ref_raw,
    own_units,
    near_units,
    text_unit,
    ref_text,
    ref_scale,
    match_rows,
    logits,
    ref_logits,
    slopes,
    near_sum,
    text_send,
    text_recv,
    image_send,
    image_recv,
    load_sem,
    half_sem,
    rt_send_sem,
    rt_recv_sem,
    im_send_sem,
    im_recv_sem,
    tg_send_sem,
    tg_recv_sem,
    ig_send_sem,
    ig_recv_sem,
    relay_out_buf,
    relay_back_buf,
    relay_in_sem,
    relay_fwd_sem,
):
    rows, depth = images.shape
    pairs = texts.shape[0]
    half = ref_texts.shape[0]
    chunks = pairs // chunk
    piece = rows // 3
    tile = 32 if piece % 128 == 0 else 16
    early = chunks // 2
    step = GROUP * tile

    dp, ref = lax.axis_index("dp"), lax.axis_index("ref")
    after, before = lax.rem(dp + 1, n), lax.rem(dp + n - 1, n)
    partner = (dp, 1 - ref)
    next_dev, prev_dev = (after, ref), (before, ref)

    def part(c):
        return pl.ds(pl.multiple_of(c * chunk, chunk), chunk)

    own_half = pl.ds(pl.multiple_of(ref * half, half), half)
    loads = [
        pltpu.make_async_copy(images, image_raw, load_sem.at[0]),
        pltpu.make_async_copy(ref_images, ref_raw, load_sem.at[1]),
        pltpu.make_async_copy(texts, text_raw, load_sem.at[2]),
        pltpu.make_async_copy(ref_texts, ref_text.at[own_half], half_sem),
    ]
    relayed = n == 2 * PLANE
    if relayed:
        place, plane = lax.rem(dp, PLANE), dp // PLANE
        here, there = plane * PLANE, (1 - plane) * PLANE
        is_first, is_last = place == 0, place == PLANE - 1

        def among(places):
            return functools.reduce(jnp.logical_or, [place == p for p in places])

        def order(places, start):
            return sum(jnp.where(place == p, start + i, 0) for i, p in enumerate(places))

        second = tuple(p + 1 for p in TWICE)
        is_pass, is_second = among(TWICE), among(second)
        is_same, is_other = among(SAME), among(OTHER)
        back_same, back_other = among(BACK_SAME), among(BACK_OTHER)
        is_back = back_same | back_other
        is_relay = is_pass | is_second | is_same | is_other | is_back
        source = jnp.where(
            is_pass | is_same,
            here,
            jnp.where(
                is_second,
                there + place - 1,
                jnp.where(
                    is_other,
                    there,
                    jnp.where(back_same, here + PLANE - 1, there + PLANE - 1),
                ),
            ),
        )
        target = jnp.where(
            is_pass,
            there + place + 1,
            jnp.where(
                is_same,
                there + PLANE - 1,
                jnp.where(
                    is_second | is_other, here + PLANE - 1, jnp.where(back_same, there, here)
                ),
            ),
        )
        source_dev, target_dev = (source, ref), (target, ref)
        out_index = order(second, 0) + order(SAME, 4) + order(OTHER, 7)
        back_index = order(BACK_SAME, 0) + order(BACK_OTHER, 3)
        first_out = [here + p for p in TWICE + SAME] + [there + p for p in OTHER]
        first_back = [there + p for p in BACK_SAME] + [here + p for p in BACK_OTHER]
        last_out = [here + p for p in second + OTHER] + [there + p for p in SAME]
        last_back = [here + p for p in BACK_SAME] + [there + p for p in BACK_OTHER]
        out_part = -(-2 * rows // (OUT_PARTS + 1) // 16) * 16
        back_part = -(-rows // 6 // 16) * 16

    barrier = pltpu.get_barrier_semaphore()

    def greet(others):
        for other in others:
            pl.semaphore_signal(barrier, inc=1, device_id=other, device_id_type=MESH)

    greet((partner, next_dev, prev_dev))
    if relayed:
        pl.when(is_first)(lambda: greet([(p, ref) for p in first_out + first_back]))
        pl.when(is_last)(lambda: greet([(p, ref) for p in last_out + last_back]))
        pl.when(is_relay)(lambda: greet((source_dev, target_dev)))
    peers = 3
    if relayed:
        ends = 3 + OUT_PARTS + BACK_PARTS
        peers = jnp.where(is_first | is_last, ends, jnp.where(is_relay, 5, 3))
    for load in loads:
        load.start()
    pl.semaphore_wait(barrier, peers)

    def rt_copy(c):
        return pltpu.make_async_remote_copy(
            src_ref=ref_texts.at[:, part(c)],
            dst_ref=ref_text.at[own_half, part(c)],
            send_sem=rt_send_sem.at[c],
            recv_sem=rt_recv_sem.at[c],
            device_id=partner,
            device_id_type=MESH,
        )

    def tg_copy(i):
        at = pl.ds(pl.multiple_of(i * step, step), step)
        return pltpu.make_async_remote_copy(
            src_ref=text_send.at[at],
            dst_ref=text_recv.at[at],
            send_sem=tg_send_sem.at[i],
            recv_sem=tg_recv_sem.at[i],
            device_id=partner,
            device_id_type=MESH,
        )

    def im_copy(k):
        at = pl.ds(k * piece, piece)
        return pltpu.make_async_remote_copy(
            src_ref=own_units.at[at],
            dst_ref=near_units.at[at],
            send_sem=im_send_sem.at[k],
            recv_sem=im_recv_sem.at[k],
            device_id=prev_dev,
            device_id_type=MESH,
        )

    ig_copy = pltpu.make_async_remote_copy(
        src_ref=image_send,
        dst_ref=image_recv,
        send_sem=ig_send_sem.at[0],
        recv_sem=ig_recv_sem.at[0],
        device_id=next_dev,
        device_id_type=MESH,
    )

    if relayed:
        out_to_relay = [
            pltpu.make_async_remote_copy(
                src_ref=own_units.at[pl.ds(m * out_part, out_part)],
                dst_ref=relay_out_buf,
                send_sem=im_send_sem.at[m],
                recv_sem=relay_in_sem,
                device_id=(first_out[m], ref),
                device_id_type=MESH,
            )
            for m in range(OUT_PARTS)
        ]
        out_rest = pl.ds(OUT_PARTS * out_part, 2 * rows - OUT_PARTS * out_part)
        out_direct = pltpu.make_async_remote_copy(
            src_ref=own_units.at[out_rest],
            dst_ref=near_units.at[out_rest],
            send_sem=im_send_sem.at[OUT_PARTS],
            recv_sem=im_recv_sem.at[OUT_PARTS],
            device_id=prev_dev,
            device_id_type=MESH,
        )

        def out_from_relay(m):
            return pltpu.make_async_remote_copy(
                src_ref=relay_out_buf,
                dst_ref=near_units.at[pl.ds(pl.multiple_of(m * out_part, 16), out_part)],
                send_sem=relay_fwd_sem,
                recv_sem=im_recv_sem.at[m],
                device_id=target_dev,
                device_id_type=MESH,
            )

        out_pass = pltpu.make_async_remote_copy(
            src_ref=relay_out_buf,
            dst_ref=relay_out_buf,
            send_sem=relay_fwd_sem,
            recv_sem=relay_in_sem,
            device_id=target_dev,
            device_id_type=MESH,
        )

        back_to_relay = [
            pltpu.make_async_remote_copy(
                src_ref=image_send.at[pl.ds(m * back_part, back_part)],
                dst_ref=relay_back_buf,
                send_sem=ig_send_sem.at[m],
                recv_sem=relay_in_sem,
                device_id=(last_back[m], ref),
                device_id_type=MESH,
            )
            for m in range(BACK_PARTS)
        ]
        back_rest = pl.ds(BACK_PARTS * back_part, rows - BACK_PARTS * back_part)
        back_direct = pltpu.make_async_remote_copy(
            src_ref=image_send.at[back_rest],
            dst_ref=image_recv.at[back_rest],
            send_sem=ig_send_sem.at[BACK_PARTS],
            recv_sem=ig_recv_sem.at[BACK_PARTS],
            device_id=next_dev,
            device_id_type=MESH,
        )

        def back_from_relay(m):
            return pltpu.make_async_remote_copy(
                src_ref=relay_back_buf,
                dst_ref=image_recv.at[pl.ds(pl.multiple_of(m * back_part, 16), back_part)],
                send_sem=relay_fwd_sem,
                recv_sem=ig_recv_sem.at[m],
                device_id=target_dev,
                device_id_type=MESH,
            )

    for c in range(chunks):
        rt_copy(c).start()

    def unit_rows(source, source_at, target, target_at, count):
        def body(start):
            scales = []
            for j in range(GROUP):
                value = source[pl.ds(source_at + start + j * tile, tile), :].astype(F32)
                scales.append(inverse_norm(row_sum(value * value)))
            for j in range(GROUP):
                value = source[pl.ds(source_at + start + j * tile, tile), :].astype(F32)
                target[pl.ds(target_at + start + j * tile, tile), :] = (value * scales[j]).astype(
                    BF16
                )

        blocks(count, GROUP * tile, body)

    def send_parts(k):
        for m in range(k * piece // out_part, min((k + 1) * piece // out_part, OUT_PARTS)):
            out_to_relay[m].start()
        if k == 5:
            out_direct.start()

    for k in range(6):
        if k % 3 == 0:
            loads[k // 3].wait()
        unit_rows(
            (image_raw, ref_raw)[k // 3], (k % 3) * piece, own_units, k * piece, piece
        )
        if relayed:
            pl.when(jnp.logical_not(is_first))(lambda: im_copy(k).start())
            pl.when(is_first)(lambda: send_parts(k))
        else:
            im_copy(k).start()

    t0, t1 = temps[0], temps[1]
    b0, b1 = biases[0], biases[1]
    over_rows = (((1,), (1,)), ((), ()))
    over_images = (((0,), (0,)), ((), ()))

    def window(units, w, c):
        at = part(c)
        logits[...] = lax.dot_general(
            units[0:rows, :], text_unit[at, :], over_rows, preferred_element_type=F32
        )
        ref_logits[...] = jnp.dot(
            units[rows : 2 * rows, :], ref_text[:, at], preferred_element_type=F32
        )
        ref_temp = ref_scale[c, 0:1, :] * t1

        def slope_rows(start):
            for j in range(GROUP):
                here = pl.ds(start + j * tile, tile)
                policy = logits[here, :] * t0
                gap = policy - ref_logits[here, :] * ref_temp + (b0 - b1)
                growth = jnp.exp2((policy + b0) * (-LOG2E))
                prob = 1.0 / (1.0 + growth)
                rest = growth * prob
                first = prob
                if w == 0:
                    columns = lax.broadcasted_iota(jnp.int32, (tile, chunk), 1) + c * chunk
                    first = jnp.where(columns == match_rows[here, :], -rest, prob)
                slopes[here, :] = (first + prob * rest * gap).astype(BF16)

        blocks(rows, GROUP * tile, slope_rows)
        total = near_sum if w else grad_images
        total[...] += jnp.dot(slopes[...], text_unit[at, :], preferred_element_type=F32)
        return lax.dot_general(
            slopes[...], units[0:rows, :], over_images, preferred_element_type=F32
        )

    match_rows[...] = jnp.broadcast_to(match[...], (chunk, rows)).T
    near_sum[...] = jnp.zeros_like(near_sum)
    grad_images[...] = jnp.zeros_like(grad_images)
    loads[2].wait()
    unit_rows(text_raw, 0, text_unit, 0, pairs)
    loads[3].wait()

    def relay_pass():
        out_to_relay[0].wait_recv()
        out_pass.start()

    def relay_out():
        out_to_relay[0].wait_recv()
        out_from_relay(out_index).start()

    def relay_back():
        back_to_relay[0].wait_recv()
        back_from_relay(back_index).start()

    def own(c, carry):
        rt_copy(c).wait_recv()
        if relayed:
            pl.when((is_other & (c == 1)) | (is_second & (c == early - 1)))(relay_out)
        value = ref_text[:, part(c)].astype(F32)
        scale = inverse_norm(jnp.sum(value * value, axis=0, keepdims=True))
        ref_scale[c] = jnp.broadcast_to(scale, (8, chunk))
        grad_texts[part(c), :] = window(own_units, 0, c)
        return carry

    if relayed:
        pl.when(is_pass)(relay_pass)
        pl.when(is_same)(relay_out)
    lax.fori_loop(0, early, own, 0)

    def wait_pieces():
        for k in range(6):
            im_copy(k).wait_recv()

    def wait_parts():
        for m in range(OUT_PARTS):
            out_from_relay(m).wait_recv()
        out_direct.wait_recv()

    if relayed:
        pl.when(is_last)(wait_parts)
        pl.when(jnp.logical_not(is_last))(wait_pieces)
    else:
        wait_pieces()

    def back_rows(read_grad, raw, out, start, divide):
        scales, alongs = [], []
        for j in range(GROUP):
            at = pl.ds(start + j * tile, tile)
            value = raw[at, :].astype(F32)
            scales.append(inverse_norm(row_sum(value * value)))
            alongs.append(row_sum(read_grad(at) * value))
        for j in range(GROUP):
            at = pl.ds(start + j * tile, tile)
            scale = scales[j]
            along = alongs[j] * scale * scale
            grad = read_grad(at) - raw[at, :].astype(F32) * along
            out[at, :] = (grad * scale if divide else grad).astype(out.dtype)

    def near(c, carry):
        grad_texts[part(c), :] = t0 * (grad_texts[part(c), :] + window(near_units, 1, c))

        def send_rows(start):
            start = pl.multiple_of(c * chunk + start, step)
            back_rows(lambda at: grad_texts[at, :], text_raw, text_send, start, False)
            tg_copy(start // step).start()

        blocks(chunk, step, send_rows)

        @pl.when(c + early < chunks)
        def _():
            own(c + early, 0)

        return carry

    lax.fori_loop(0, chunks, near, 0)

    def cast_rows(start):
        for j in range(GROUP):
            at = pl.ds(start + j * tile, tile)
            grad = t0 * near_sum[at, :]
            unit = near_units[at, :].astype(F32)
            along = row_sum(grad * unit)
            image_send[at, :] = (grad - unit * (along * (1.0 - KEEP))).astype(BF16)

    def received(at):
        grad = image_recv[at, :].astype(F32)
        unit = own_units[at, :].astype(F32)
        return grad + unit * (row_sum(grad * unit) * (1.0 / KEEP - 1.0))

    blocks(rows, GROUP * tile, cast_rows)

    def start_back():
        for copy in back_to_relay:
            copy.start()
        back_direct.start()

    def wait_back():
        for m in range(BACK_PARTS):
            back_from_relay(m).wait_recv()
        back_direct.wait_recv()

    if relayed:
        pl.when(is_last)(start_back)
        pl.when(jnp.logical_not(is_last))(lambda: ig_copy.start())
        pl.when(is_back)(relay_back)
    else:
        ig_copy.start()

    if relayed:
        pl.when(is_first)(wait_back)
        pl.when(jnp.logical_not(is_first))(lambda: ig_copy.wait_recv())
    else:
        ig_copy.wait_recv()
    blocks(
        rows,
        GROUP * tile,
        lambda start: back_rows(
            lambda at: t0 * grad_images[at, :] + received(at),
            image_raw,
            grad_images,
            start,
            True,
        ),
    )

    def finish(i, carry):
        tg_copy(i).wait_recv()
        back_rows(
            lambda at: text_send[at, :].astype(F32) + text_recv[at, :].astype(F32),
            text_raw,
            grad_texts,
            pl.multiple_of(i * step, step),
            True,
        )
        return carry

    lax.fori_loop(0, pairs // step, finish, 0)

    def sent_pieces():
        for k in range(6):
            im_copy(k).wait_send()

    def sent_parts():
        for copy in out_to_relay:
            copy.wait_send()
        out_direct.wait_send()

    def sent_back():
        for copy in back_to_relay:
            copy.wait_send()
        back_direct.wait_send()

    if relayed:
        pl.when(is_first)(sent_parts)
        pl.when(jnp.logical_not(is_first))(sent_pieces)
        pl.when(is_last)(sent_back)
        pl.when(jnp.logical_not(is_last))(lambda: ig_copy.wait_send())
        pl.when(is_pass)(lambda: out_pass.wait_send())
        pl.when(is_same | is_other | is_second)(lambda: out_from_relay(out_index).wait_send())
        pl.when(is_back)(lambda: back_from_relay(back_index).wait_send())
    else:
        sent_pieces()
        ig_copy.wait_send()

    def drain(c, carry):
        rt_copy(c).wait_send()
        return carry

    lax.fori_loop(0, chunks, drain, 0)

    def sent_texts(i, carry):
        tg_copy(i).wait_send()
        return carry

    lax.fori_loop(0, pairs // step, sent_texts, 0)


def write_out(split, images_in, texts_in, images_out, texts_out, sem):
    copies = []
    for source, target in ((texts_in, texts_out), (images_in, images_out)):
        count = source.shape[0] // split
        for i in range(split):
            at = pl.ds(i * count, count)
            copies.append(
                pltpu.make_async_copy(source.at[at], target.at[at], sem.at[len(copies)])
            )
    for copy in copies:
        copy.start()
    for copy in copies:
        copy.wait()


def per_device(n, images, texts, ref_images, ref_texts, positives, temps, biases):
    rows, depth = images.shape
    pairs, half = ref_texts.shape
    chunk = 256 if pairs % 256 == 0 else pairs // 2
    chunks = pairs // chunk
    text_parts = pairs // (GROUP * (32 if rows // 3 % 128 == 0 else 16))
    anywhere = pl.BlockSpec(memory_space=pl.ANY)
    scalars = pl.BlockSpec(memory_space=pltpu.SMEM)
    dma = pltpu.SemaphoreType.DMA
    grad_images, grad_texts = pl.pallas_call(
        functools.partial(kernel, n, chunk),
        out_shape=(
            pltpu.VMEM((rows, depth), F32),
            pltpu.VMEM((pairs, depth), F32),
        ),
        in_specs=[anywhere] * 4 + [pl.BlockSpec(memory_space=pltpu.VMEM), scalars, scalars],
        out_specs=(pl.BlockSpec(memory_space=pltpu.VMEM), pl.BlockSpec(memory_space=pltpu.VMEM)),
        scratch_shapes=[
            pltpu.VMEM((rows, depth), BF16),
            pltpu.VMEM((pairs, depth), BF16),
            pltpu.VMEM((rows, depth), BF16),
            pltpu.VMEM((2 * rows, depth), BF16),
            pltpu.VMEM((2 * rows, depth), BF16),
            pltpu.VMEM((pairs, depth), BF16),
            pltpu.VMEM((depth, pairs), BF16),
            pltpu.VMEM((chunks, 8, chunk), F32),
            pltpu.VMEM((rows, chunk), jnp.int32),
            pltpu.VMEM((rows, chunk), F32),
            pltpu.VMEM((rows, chunk), F32),
            pltpu.VMEM((rows, chunk), BF16),
            pltpu.VMEM((rows, depth), F32),
            pltpu.VMEM((pairs, depth), BF16),
            pltpu.VMEM((pairs, depth), BF16),
            pltpu.VMEM((rows, depth), BF16),
            pltpu.VMEM((rows, depth), BF16),
            dma((3,)),
            dma,
            dma((chunks,)),
            dma((chunks,)),
            dma((OUT_PARTS + 1,)),
            dma((OUT_PARTS + 1,)),
            dma((text_parts,)),
            dma((text_parts,)),
            dma((BACK_PARTS + 1,)),
            dma((BACK_PARTS + 1,)),
            pltpu.VMEM((-(-2 * rows // (OUT_PARTS + 1) // 16) * 16, depth), BF16),
            pltpu.VMEM((-(-rows // 6 // 16) * 16, depth), BF16),
            dma,
            dma,
        ],
        compiler_params=pltpu.CompilerParams(
            collective_id=0, has_side_effects=True, vmem_limit_bytes=50 * 1024 * 1024
        ),
        cost_estimate=pl.CostEstimate(
            flops=16 * rows * pairs * depth,
            bytes_accessed=12 * pairs * depth,
            transcendentals=4 * rows * pairs,
        ),
    )(images, texts, ref_images, ref_texts.T, positives, temps, biases)
    split = 4
    return pl.pallas_call(
        functools.partial(write_out, split),
        out_shape=(
            jax.ShapeDtypeStruct((rows, depth), F32),
            jax.ShapeDtypeStruct((pairs, depth), F32),
        ),
        in_specs=[pl.BlockSpec(memory_space=pltpu.VMEM)] * 2,
        out_specs=(anywhere, anywhere),
        scratch_shapes=[dma((2 * split,))],
        compiler_params=pltpu.CompilerParams(vmem_limit_bytes=4 * 1024 * 1024),
        cost_estimate=pl.CostEstimate(
            flops=0, bytes_accessed=8 * (rows + pairs) * depth, transcendentals=0
        ),
    )(
        pltpu.with_memory_space_constraint(grad_images, pltpu.VMEM),
        pltpu.with_memory_space_constraint(grad_texts, pltpu.VMEM),
    )


def solution(mesh):
    return jax.shard_map(
        functools.partial(per_device, mesh.shape["dp"]),
        mesh=mesh,
        in_specs=(
            P(("dp", "ref"), None),
            P("dp", None),
            P(("dp", "ref"), None),
            P("dp", "ref"),
            P("dp", "ref"),
            P(),
            P(),
        ),
        out_specs=(P(("dp", "ref"), None), P("dp", None)),
        check_vma=False,
    )
```

```python
import functools

import jax
import jax.numpy as jnp
from jax import lax
from jax.experimental import pallas as pl
from jax.experimental.pallas import tpu as pltpu
from jax.sharding import PartitionSpec as P

EPS = 1e-06
MESH = pl.DeviceIdType.MESH
LOG2E = 1.4426950408889634
F32 = jnp.float32
BF16 = jnp.bfloat16
GROUP = 4
KEEP = 0.0625

PLANE = 32
TWICE, SAME, OTHER = (10, 18, 12, 20), (3, 5, 7), (8, 16)
BACK_SAME, BACK_OTHER = (26, 28), (14, 22)
OUT_PARTS, BACK_PARTS = 9, 4


def blocks(count, size, body):
    def step(i, carry):
        body(pl.multiple_of(i * size, size))
        return carry

    lax.fori_loop(0, count // size, step, 0)


def inverse_norm(square_sum):
    return lax.rsqrt(square_sum + EPS)


def row_sum(value):
    return jnp.sum(value, axis=-1, keepdims=True)


def kernel(
    n,
    chunk,
    images,
    texts,
    ref_images,
    ref_texts,
    match,
    temps,
    biases,
    grad_images,
    grad_texts,
    image_raw,
    text_raw,
    ref_raw,
    own_units,
    near_units,
    text_unit,
    ref_text,
    ref_scale,
    match_rows,
    logits,
    ref_logits,
    slopes,
    near_sum,
    text_send,
    text_recv,
    image_send,
    image_recv,
    load_sem,
    half_sem,
    rt_send_sem,
    rt_recv_sem,
    im_send_sem,
    im_recv_sem,
    tg_send_sem,
    tg_recv_sem,
    ig_send_sem,
    ig_recv_sem,
    relay_out_buf,
    relay_back_buf,
    relay_in_sem,
    relay_fwd_sem,
):
    rows, depth = images.shape
    pairs = texts.shape[0]
    half = ref_texts.shape[0]
    chunks = pairs // chunk
    piece = rows // 3
    tile = 32 if piece % 128 == 0 else 16
    early = chunks // 2

    dp, ref = lax.axis_index("dp"), lax.axis_index("ref")
    after, before = lax.rem(dp + 1, n), lax.rem(dp + n - 1, n)
    partner = (dp, 1 - ref)
    next_dev, prev_dev = (after, ref), (before, ref)

    def part(c):
        return pl.ds(pl.multiple_of(c * chunk, chunk), chunk)

    own_half = pl.ds(pl.multiple_of(ref * half, half), half)
    loads = [
        pltpu.make_async_copy(images, image_raw, load_sem.at[0]),
        pltpu.make_async_copy(ref_images, ref_raw, load_sem.at[1]),
        pltpu.make_async_copy(texts, text_raw, load_sem.at[2]),
        pltpu.make_async_copy(ref_texts, ref_text.at[own_half], half_sem),
    ]
    relayed = n == 2 * PLANE
    if relayed:
        place, plane = lax.rem(dp, PLANE), dp // PLANE
        here, there = plane * PLANE, (1 - plane) * PLANE
        is_first, is_last = place == 0, place == PLANE - 1

        def among(places):
            return functools.reduce(jnp.logical_or, [place == p for p in places])

        def order(places, start):
            return sum(jnp.where(place == p, start + i, 0) for i, p in enumerate(places))

        second = tuple(p + 1 for p in TWICE)
        is_pass, is_second = among(TWICE), among(second)
        is_same, is_other = among(SAME), among(OTHER)
        back_same, back_other = among(BACK_SAME), among(BACK_OTHER)
        is_back = back_same | back_other
        is_relay = is_pass | is_second | is_same | is_other | is_back
        source = jnp.where(
            is_pass | is_same,
            here,
            jnp.where(
                is_second,
                there + place - 1,
                jnp.where(
                    is_other,
                    there,
                    jnp.where(back_same, here + PLANE - 1, there + PLANE - 1),
                ),
            ),
        )
        target = jnp.where(
            is_pass,
            there + place + 1,
            jnp.where(
                is_same,
                there + PLANE - 1,
                jnp.where(
                    is_second | is_other, here + PLANE - 1, jnp.where(back_same, there, here)
                ),
            ),
        )
        source_dev, target_dev = (source, ref), (target, ref)
        out_index = order(second, 0) + order(SAME, 4) + order(OTHER, 7)
        back_index = order(BACK_SAME, 0) + order(BACK_OTHER, 2)
        first_out = [here + p for p in TWICE + SAME] + [there + p for p in OTHER]
        first_back = [there + p for p in BACK_SAME] + [here + p for p in BACK_OTHER]
        last_out = [here + p for p in second + OTHER] + [there + p for p in SAME]
        last_back = [here + p for p in BACK_SAME] + [there + p for p in BACK_OTHER]
        out_part = -(-2 * rows // (OUT_PARTS + 1) // 16) * 16
        back_part = -(-rows // 5 // 16) * 16

    barrier = pltpu.get_barrier_semaphore()

    def greet(others):
        for other in others:
            pl.semaphore_signal(barrier, inc=1, device_id=other, device_id_type=MESH)

    greet((partner, next_dev, prev_dev))
    if relayed:
        pl.when(is_first)(lambda: greet([(p, ref) for p in first_out + first_back]))
        pl.when(is_last)(lambda: greet([(p, ref) for p in last_out + last_back]))
        pl.when(is_relay)(lambda: greet((source_dev, target_dev)))
    peers = 3
    if relayed:
        ends = 3 + OUT_PARTS + BACK_PARTS
        peers = jnp.where(is_first | is_last, ends, jnp.where(is_relay, 5, 3))
    for load in loads:
        load.start()
    pl.semaphore_wait(barrier, peers)

    def rt_copy(c):
        return pltpu.make_async_remote_copy(
            src_ref=ref_texts.at[:, part(c)],
            dst_ref=ref_text.at[own_half, part(c)],
            send_sem=rt_send_sem.at[c],
            recv_sem=rt_recv_sem.at[c],
            device_id=partner,
            device_id_type=MESH,
        )

    def tg_copy(c):
        return pltpu.make_async_remote_copy(
            src_ref=text_send.at[part(c)],
            dst_ref=text_recv.at[part(c)],
            send_sem=tg_send_sem.at[c],
            recv_sem=tg_recv_sem.at[c],
            device_id=partner,
            device_id_type=MESH,
        )

    def im_copy(k):
        at = pl.ds(k * piece, piece)
        return pltpu.make_async_remote_copy(
            src_ref=own_units.at[at],
            dst_ref=near_units.at[at],
            send_sem=im_send_sem.at[k],
            recv_sem=im_recv_sem.at[k],
            device_id=prev_dev,
            device_id_type=MESH,
        )

    ig_copy = pltpu.make_async_remote_copy(
        src_ref=image_send,
        dst_ref=image_recv,
        send_sem=ig_send_sem.at[0],
        recv_sem=ig_recv_sem.at[0],
        device_id=next_dev,
        device_id_type=MESH,
    )

    if relayed:
        out_to_relay = [
            pltpu.make_async_remote_copy(
                src_ref=own_units.at[pl.ds(m * out_part, out_part)],
                dst_ref=relay_out_buf,
                send_sem=im_send_sem.at[m],
                recv_sem=relay_in_sem,
                device_id=(first_out[m], ref),
                device_id_type=MESH,
            )
            for m in range(OUT_PARTS)
        ]
        out_rest = pl.ds(OUT_PARTS * out_part, 2 * rows - OUT_PARTS * out_part)
        out_direct = pltpu.make_async_remote_copy(
            src_ref=own_units.at[out_rest],
            dst_ref=near_units.at[out_rest],
            send_sem=im_send_sem.at[OUT_PARTS],
            recv_sem=im_recv_sem.at[OUT_PARTS],
            device_id=prev_dev,
            device_id_type=MESH,
        )

        def out_from_relay(m):
            return pltpu.make_async_remote_copy(
                src_ref=relay_out_buf,
                dst_ref=near_units.at[pl.ds(pl.multiple_of(m * out_part, 16), out_part)],
                send_sem=relay_fwd_sem,
                recv_sem=im_recv_sem.at[m],
                device_id=target_dev,
                device_id_type=MESH,
            )

        out_pass = pltpu.make_async_remote_copy(
            src_ref=relay_out_buf,
            dst_ref=relay_out_buf,
            send_sem=relay_fwd_sem,
            recv_sem=relay_in_sem,
            device_id=target_dev,
            device_id_type=MESH,
        )

        back_to_relay = [
            pltpu.make_async_remote_copy(
                src_ref=image_send.at[pl.ds(m * back_part, back_part)],
                dst_ref=relay_back_buf,
                send_sem=ig_send_sem.at[m],
                recv_sem=relay_in_sem,
                device_id=(last_back[m], ref),
                device_id_type=MESH,
            )
            for m in range(BACK_PARTS)
        ]
        back_rest = pl.ds(BACK_PARTS * back_part, rows - BACK_PARTS * back_part)
        back_direct = pltpu.make_async_remote_copy(
            src_ref=image_send.at[back_rest],
            dst_ref=image_recv.at[back_rest],
            send_sem=ig_send_sem.at[BACK_PARTS],
            recv_sem=ig_recv_sem.at[BACK_PARTS],
            device_id=next_dev,
            device_id_type=MESH,
        )

        def back_from_relay(m):
            return pltpu.make_async_remote_copy(
                src_ref=relay_back_buf,
                dst_ref=image_recv.at[pl.ds(pl.multiple_of(m * back_part, 16), back_part)],
                send_sem=relay_fwd_sem,
                recv_sem=ig_recv_sem.at[m],
                device_id=target_dev,
                device_id_type=MESH,
            )

    for c in range(chunks):
        rt_copy(c).start()

    def unit_rows(source, source_at, target, target_at, count):
        def body(start):
            scales = []
            for j in range(GROUP):
                value = source[pl.ds(source_at + start + j * tile, tile), :].astype(F32)
                scales.append(inverse_norm(row_sum(value * value)))
            for j in range(GROUP):
                value = source[pl.ds(source_at + start + j * tile, tile), :].astype(F32)
                target[pl.ds(target_at + start + j * tile, tile), :] = (value * scales[j]).astype(
                    BF16
                )

        blocks(count, GROUP * tile, body)

    def send_parts(k):
        for m in range(k * piece // out_part, min((k + 1) * piece // out_part, OUT_PARTS)):
            out_to_relay[m].start()
        if k == 5:
            out_direct.start()

    for k in range(6):
        if k % 3 == 0:
            loads[k // 3].wait()
        unit_rows(
            (image_raw, ref_raw)[k // 3], (k % 3) * piece, own_units, k * piece, piece
        )
        if relayed:
            pl.when(jnp.logical_not(is_first))(lambda: im_copy(k).start())
            pl.when(is_first)(lambda: send_parts(k))
        else:
            im_copy(k).start()

    t0, t1 = temps[0], temps[1]
    b0, b1 = biases[0], biases[1]
    over_rows = (((1,), (1,)), ((), ()))
    over_images = (((0,), (0,)), ((), ()))

    def window(units, w, c):
        at = part(c)
        logits[...] = lax.dot_general(
            units[0:rows, :], text_unit[at, :], over_rows, preferred_element_type=F32
        )
        ref_logits[...] = jnp.dot(
            units[rows : 2 * rows, :], ref_text[:, at], preferred_element_type=F32
        )
        ref_temp = ref_scale[c, 0:1, :] * t1

        def slope_rows(start):
            for j in range(GROUP):
                here = pl.ds(start + j * tile, tile)
                policy = logits[here, :] * t0
                gap = policy - ref_logits[here, :] * ref_temp + (b0 - b1)
                growth = jnp.exp2((policy + b0) * (-LOG2E))
                prob = 1.0 / (1.0 + growth)
                rest = growth * prob
                first = prob
                if w == 0:
                    columns = lax.broadcasted_iota(jnp.int32, (tile, chunk), 1) + c * chunk
                    first = jnp.where(columns == match_rows[here, :], -rest, prob)
                slopes[here, :] = (first + prob * rest * gap).astype(BF16)

        blocks(rows, GROUP * tile, slope_rows)
        total = near_sum if w else grad_images
        total[...] += jnp.dot(slopes[...], text_unit[at, :], preferred_element_type=F32)
        return lax.dot_general(
            slopes[...], units[0:rows, :], over_images, preferred_element_type=F32
        )

    match_rows[...] = jnp.broadcast_to(match[...], (chunk, rows)).T
    near_sum[...] = jnp.zeros_like(near_sum)
    grad_images[...] = jnp.zeros_like(grad_images)
    loads[2].wait()
    unit_rows(text_raw, 0, text_unit, 0, pairs)
    loads[3].wait()

    def relay_pass():
        out_to_relay[0].wait_recv()
        out_pass.start()

    def relay_out():
        out_to_relay[0].wait_recv()
        out_from_relay(out_index).start()

    def relay_back():
        back_to_relay[0].wait_recv()
        back_from_relay(back_index).start()

    def own(c, carry):
        rt_copy(c).wait_recv()
        if relayed:
            pl.when((is_other & (c == 1)) | (is_second & (c == early - 1)))(relay_out)
        value = ref_text[:, part(c)].astype(F32)
        scale = inverse_norm(jnp.sum(value * value, axis=0, keepdims=True))
        ref_scale[c] = jnp.broadcast_to(scale, (8, chunk))
        grad_texts[part(c), :] = window(own_units, 0, c)
        return carry

    if relayed:
        pl.when(is_pass)(relay_pass)
        pl.when(is_same)(relay_out)
    lax.fori_loop(0, early, own, 0)

    def wait_pieces():
        for k in range(6):
            im_copy(k).wait_recv()

    def wait_parts():
        for m in range(OUT_PARTS):
            out_from_relay(m).wait_recv()
        out_direct.wait_recv()

    if relayed:
        pl.when(is_last)(wait_parts)
        pl.when(jnp.logical_not(is_last))(wait_pieces)
    else:
        wait_pieces()

    def back_rows(read_grad, raw, out, start, divide):
        scales, alongs = [], []
        for j in range(GROUP):
            at = pl.ds(start + j * tile, tile)
            value = raw[at, :].astype(F32)
            scales.append(inverse_norm(row_sum(value * value)))
            alongs.append(row_sum(read_grad(at) * value))
        for j in range(GROUP):
            at = pl.ds(start + j * tile, tile)
            scale = scales[j]
            along = alongs[j] * scale * scale
            grad = read_grad(at) - raw[at, :].astype(F32) * along
            out[at, :] = (grad * scale if divide else grad).astype(out.dtype)

    def near(c, carry):
        grad_texts[part(c), :] = t0 * (grad_texts[part(c), :] + window(near_units, 1, c))
        blocks(
            chunk,
            GROUP * tile,
            lambda start: back_rows(
                lambda at: grad_texts[at, :],
                text_raw,
                text_send,
                pl.multiple_of(c * chunk + start, GROUP * tile),
                False,
            ),
        )
        tg_copy(c).start()

        @pl.when(c + early < chunks)
        def _():
            own(c + early, 0)

        return carry

    lax.fori_loop(0, chunks, near, 0)

    def cast_rows(start):
        for j in range(GROUP):
            at = pl.ds(start + j * tile, tile)
            grad = t0 * near_sum[at, :]
            unit = near_units[at, :].astype(F32)
            along = row_sum(grad * unit)
            image_send[at, :] = (grad - unit * (along * (1.0 - KEEP))).astype(BF16)

    def received(at):
        grad = image_recv[at, :].astype(F32)
        unit = own_units[at, :].astype(F32)
        return grad + unit * (row_sum(grad * unit) * (1.0 / KEEP - 1.0))

    blocks(rows, GROUP * tile, cast_rows)

    def start_back():
        for copy in back_to_relay:
            copy.start()
        back_direct.start()

    def wait_back():
        for m in range(BACK_PARTS):
            back_from_relay(m).wait_recv()
        back_direct.wait_recv()

    if relayed:
        pl.when(is_last)(start_back)
        pl.when(jnp.logical_not(is_last))(lambda: ig_copy.start())
        pl.when(is_back)(relay_back)
    else:
        ig_copy.start()

    if relayed:
        pl.when(is_first)(wait_back)
        pl.when(jnp.logical_not(is_first))(lambda: ig_copy.wait_recv())
    else:
        ig_copy.wait_recv()
    blocks(
        rows,
        GROUP * tile,
        lambda start: back_rows(
            lambda at: t0 * grad_images[at, :] + received(at),
            image_raw,
            grad_images,
            start,
            True,
        ),
    )

    def sent_pieces():
        for k in range(6):
            im_copy(k).wait_send()

    def sent_parts():
        for copy in out_to_relay:
            copy.wait_send()
        out_direct.wait_send()

    def sent_back():
        for copy in back_to_relay:
            copy.wait_send()
        back_direct.wait_send()

    if relayed:
        pl.when(is_first)(sent_parts)
        pl.when(jnp.logical_not(is_first))(sent_pieces)
        pl.when(is_last)(sent_back)
        pl.when(jnp.logical_not(is_last))(lambda: ig_copy.wait_send())
        pl.when(is_pass)(lambda: out_pass.wait_send())
        pl.when(is_same | is_other | is_second)(lambda: out_from_relay(out_index).wait_send())
        pl.when(is_back)(lambda: back_from_relay(back_index).wait_send())
    else:
        sent_pieces()
        ig_copy.wait_send()

    def finish(c, carry):
        rt_copy(c).wait_send()
        tg_copy(c).wait_send()
        tg_copy(c).wait_recv()
        blocks(
            chunk,
            GROUP * tile,
            lambda start: back_rows(
                lambda at: text_send[at, :].astype(F32) + text_recv[at, :].astype(F32),
                text_raw,
                grad_texts,
                pl.multiple_of(c * chunk + start, GROUP * tile),
                True,
            ),
        )
        return carry

    lax.fori_loop(0, chunks, finish, 0)


def write_out(split, images_in, texts_in, images_out, texts_out, sem):
    copies = []
    for source, target in ((texts_in, texts_out), (images_in, images_out)):
        count = source.shape[0] // split
        for i in range(split):
            at = pl.ds(i * count, count)
            copies.append(
                pltpu.make_async_copy(source.at[at], target.at[at], sem.at[len(copies)])
            )
    for copy in copies:
        copy.start()
    for copy in copies:
        copy.wait()


def per_device(n, images, texts, ref_images, ref_texts, positives, temps, biases):
    rows, depth = images.shape
    pairs, half = ref_texts.shape
    chunk = 256 if pairs % 256 == 0 else pairs // 2
    chunks = pairs // chunk
    anywhere = pl.BlockSpec(memory_space=pl.ANY)
    scalars = pl.BlockSpec(memory_space=pltpu.SMEM)
    dma = pltpu.SemaphoreType.DMA
    grad_images, grad_texts = pl.pallas_call(
        functools.partial(kernel, n, chunk),
        out_shape=(
            pltpu.VMEM((rows, depth), F32),
            pltpu.VMEM((pairs, depth), F32),
        ),
        in_specs=[anywhere] * 4 + [pl.BlockSpec(memory_space=pltpu.VMEM), scalars, scalars],
        out_specs=(pl.BlockSpec(memory_space=pltpu.VMEM), pl.BlockSpec(memory_space=pltpu.VMEM)),
        scratch_shapes=[
            pltpu.VMEM((rows, depth), BF16),
            pltpu.VMEM((pairs, depth), BF16),
            pltpu.VMEM((rows, depth), BF16),
            pltpu.VMEM((2 * rows, depth), BF16),
            pltpu.VMEM((2 * rows, depth), BF16),
            pltpu.VMEM((pairs, depth), BF16),
            pltpu.VMEM((depth, pairs), BF16),
            pltpu.VMEM((chunks, 8, chunk), F32),
            pltpu.VMEM((rows, chunk), jnp.int32),
            pltpu.VMEM((rows, chunk), F32),
            pltpu.VMEM((rows, chunk), F32),
            pltpu.VMEM((rows, chunk), BF16),
            pltpu.VMEM((rows, depth), F32),
            pltpu.VMEM((pairs, depth), BF16),
            pltpu.VMEM((pairs, depth), BF16),
            pltpu.VMEM((rows, depth), BF16),
            pltpu.VMEM((rows, depth), BF16),
            dma((3,)),
            dma,
            dma((chunks,)),
            dma((chunks,)),
            dma((OUT_PARTS + 1,)),
            dma((OUT_PARTS + 1,)),
            dma((chunks,)),
            dma((chunks,)),
            dma((BACK_PARTS + 1,)),
            dma((BACK_PARTS + 1,)),
            pltpu.VMEM((-(-2 * rows // (OUT_PARTS + 1) // 16) * 16, depth), BF16),
            pltpu.VMEM((-(-rows // 5 // 16) * 16, depth), BF16),
            dma,
            dma,
        ],
        compiler_params=pltpu.CompilerParams(
            collective_id=0, has_side_effects=True, vmem_limit_bytes=50 * 1024 * 1024
        ),
        cost_estimate=pl.CostEstimate(
            flops=16 * rows * pairs * depth,
            bytes_accessed=12 * pairs * depth,
            transcendentals=4 * rows * pairs,
        ),
    )(images, texts, ref_images, ref_texts.T, positives, temps, biases)
    split = 4
    return pl.pallas_call(
        functools.partial(write_out, split),
        out_shape=(
            jax.ShapeDtypeStruct((rows, depth), F32),
            jax.ShapeDtypeStruct((pairs, depth), F32),
        ),
        in_specs=[pl.BlockSpec(memory_space=pltpu.VMEM)] * 2,
        out_specs=(anywhere, anywhere),
        scratch_shapes=[dma((2 * split,))],
        compiler_params=pltpu.CompilerParams(vmem_limit_bytes=4 * 1024 * 1024),
        cost_estimate=pl.CostEstimate(
            flops=0, bytes_accessed=8 * (rows + pairs) * depth, transcendentals=0
        ),
    )(
        pltpu.with_memory_space_constraint(grad_images, pltpu.VMEM),
        pltpu.with_memory_space_constraint(grad_texts, pltpu.VMEM),
    )


def solution(mesh):
    return jax.shard_map(
        functools.partial(per_device, mesh.shape["dp"]),
        mesh=mesh,
        in_specs=(
            P(("dp", "ref"), None),
            P("dp", None),
            P(("dp", "ref"), None),
            P("dp", "ref"),
            P("dp", "ref"),
            P(),
            P(),
        ),
        out_specs=(P(("dp", "ref"), None), P("dp", None)),
        check_vma=False,
    )
```
